32 devices in a mesh: seq: 8 (over z, y), head: 4 (over x, core).
Axes of the slice: x: 2, y: 2, z: 4, core: 2. Of those that a mesh axis runs over, the one named last changes fastest.
Arguments:
- tokens: bfloat16 [8192, 2048], P('seq'), may hold values from -6 to 6
- codebook: bfloat16 [1024, 2048], replicated, may hold values from -6 to 6
- codes: int32 [8192], P('seq'), may hold values from 0 to 1023
- modality: int32 [8192], P('seq'), may hold values from 0 to 2, as said below
- segments: int32 [8, 1024], P('seq'), may hold values from 0 to 7, never falling along the last dimension, each value on 1 to 512 neighbouring positions
- sequence_source: int32 [8192], replicated, may hold values from 0 to 8191, as said below
- w_qkv: bfloat16 [2048, 3, 2048], P(None, None, 'head'), may hold values from -0.125 to 0.125
- w_out: bfloat16 [2048, 2048], P('head'), may hold values from -1 to 1
- w_up: bfloat16 [2048, 8192], P(None, 'head'), may hold values from -0.125 to 0.125
- w_down: bfloat16 [8192, 2048], P('head'), may hold values from -0.0625 to 0.0625
- norm1_gain: float32 [2048], replicated, may hold values from 0.1 to 1.9
- norm1_shift: float32 [2048], replicated, may hold values from -4 to 4
- norm2_gain: float32 [2048], replicated, may hold values from 0.1 to 1.9
- norm2_shift: float32 [2048], replicated, may hold values from -4 to 4
- cotangent: bfloat16 [8192, 2048], P('seq'), may hold values from -6 to 6
Outputs:
- block_output: bfloat16 [8192, 2048], P('seq')
- input_grad: bfloat16 [8192, 2048], P('seq')
- qkv_grad: float32 [2048, 3, 2048], P('seq', None, 'head')
- out_grad: float32 [2048, 2048], P('head', 'seq')
- up_grad: float32 [2048, 8192], P('seq', 'head')
- down_grad: float32 [8192, 2048], P('head', 'seq')
- gain_one_grad: float32 [2048], P('seq')
- shift_one_grad: float32 [2048], P('seq')
- gain_two_grad: float32 [2048], P('seq')
- shift_two_grad: float32 [2048], P('seq')
The draws below stay inside these ranges and needn't reach their ends.
Inputs may be any that keep to these rules, and one draw needn't show every extreme that they name: `modality`: never falls along the tokens. `sequence_source`: A permutation of the 8192 grouped indices. Of the 1024 positions of each packed row, exactly 128 name grouped indices of each aligned block of 1024 grouped indices.
All inputs are finite; a program needn't handle non-finite values.
Results may differ from the reference program's by a relative error of at most 0.013.
Values may be sent and summed in bfloat16 or wider, within the bound.
No kernel may reach another device: no remote copies, remote signals or barrier semaphores. Data moves between devices by JAX's collectives and lax.ppermute only.
A program may use at most 256 MiB of HBM per device.

```python
import math
import jax
import jax.numpy as jnp
import numpy as np
from jax import lax

D = 2048
HEADS = 16
HEAD_DIM = 128
FF = 8192
CODES = 1024
TOK_DEV = 1024
PER_PEER = 128
TOKENS = 8192
N_SEQ = 8


def draw_modality(key, part):
    key = jax.random.fold_in(key, 5)
    return jnp.sort(jax.random.randint(key, (TOKENS,), 0, 3)).astype(jnp.int32)


def draw_sequence_source(key, part):
    key = jax.random.fold_in(key, 7)
    first, second = jax.random.split(key)
    pattern = jnp.repeat(jnp.arange(N_SEQ, dtype=jnp.int32), PER_PEER)
    row_keys = jax.random.split(first, N_SEQ)
    anchor = jax.vmap(lambda each: jax.random.permutation(each, pattern))(row_keys).reshape(TOKENS)
    grouped = jnp.argsort(anchor, stable=True).astype(jnp.int32)
    local_keys = jax.random.split(second, N_SEQ)
    shuffled = jax.vmap(lambda each: jax.random.permutation(each, TOK_DEV))(local_keys).reshape(TOKENS).astype(jnp.int32)
    target = jnp.arange(TOKENS, dtype=jnp.int32) // TOK_DEV * TOK_DEV + shuffled
    return jnp.zeros((TOKENS,), jnp.int32).at[grouped].set(target)


def place_ends(array, own_key, least, high):
    place = [jax.random.randint(jax.random.fold_in(own_key, axis), (), 0, length) for axis, length in enumerate(array.shape)]
    widest = array.shape.index(max(array.shape))
    next_to = place[:widest] + [(place[widest] + 1) % array.shape[widest]] + place[widest + 1:]
    return array.at[tuple(place)].set(least).at[tuple(next_to)].set(high)


def with_spikes(array, own_key, source, target, blocks, factor):
    owner, partner = [(jnp.arange(array.shape[dim]) // (array.shape[dim] // blocks)).reshape([-1 if axis == dim else 1 for axis in range(array.ndim)]) for dim in (source, target)]
    chosen = jax.random.permutation(own_key, blocks)[partner]
    strong = (owner == chosen) | (owner == (partner + blocks // 2) % blocks)
    return jnp.where(strong, factor * array, array)


def steps_of(own_key, dims, pieces, smallest, largest):
    def one(position, shards_of):
        heights = jax.random.uniform(jax.random.fold_in(jax.random.fold_in(own_key, 6), position), (shards_of,), jnp.float32, smallest / len(pieces), largest / len(pieces))
        return jnp.repeat(jnp.exp(heights), dims[position] // shards_of).reshape((-1,) + (1,) * (len(dims) - position - 1))

    loudness = one(*pieces[0])
    for cut in pieces[1:]:
        loudness = loudness * one(*cut)
    return loudness


def split_up(count, total, reach, lean):
    loads = [(1 << 20) // math.isqrt(standing ** lean) + 1 for standing in range(2, count + 1)]
    spare, holding = total - reach - (count - 1), [1] * (count - 1)
    while spare > 0:
        movable = [i for i in range(count - 1) if holding[i] < reach]
        whole, left = sum([loads[i] for i in movable]), spare
        for i in movable:
            more = min(reach - holding[i], max(1, left * loads[i] // whole), spare)
            holding[i] = holding[i] + more
            spare = spare - more
    return np.array([reach] + holding)


def ragged_sizes(own_key, amount, total, most, lean):
    if amount == 2:
        one = jax.random.randint(own_key, (), max(1, total - most), min(most, total - 1) + 1)
        return jnp.stack([one, total - one])
    lengths = jnp.asarray(split_up(amount, total, most, lean), jnp.int32)
    couples = (amount - 1) // 2
    donor, sink = lengths[1:1 + 2 * couples:2], lengths[2:2 + 2 * couples:2]
    slack = jnp.minimum(donor - 1, most - sink)
    shifted = jax.random.randint(jax.random.fold_in(own_key, 1), (couples,), 0, 1 << 20) % (slack + 1)
    lengths = lengths.at[1:1 + 2 * couples:2].set(donor - shifted).at[2:2 + 2 * couples:2].set(sink + shifted)
    return lengths[jax.random.permutation(jax.random.fold_in(own_key, 2), amount)]


def normal_values(stream_key, extent, deviation, bound, cuts=(), kind=jnp.bfloat16):
    array = deviation * jax.random.normal(stream_key, extent, jnp.float32)
    if cuts:
        array = array * steps_of(stream_key, extent, cuts, -0.22, 0.18)
    return jnp.clip(array, -bound, bound).astype(kind)


def gaussian_with(own_key, dims, scale, most, shards, heavy, kind=jnp.bfloat16):
    array = scale * jax.random.normal(own_key, dims, jnp.float32)
    if shards:
        array = array * steps_of(own_key, dims, shards, -0.22, 0.18)
    return jnp.clip(with_spikes(array, jax.random.fold_in(own_key, 3), *heavy), -most, most).astype(kind)


def setup_inputs(seed: int = 0) -> dict:
    streams_of = jax.random.split(jax.random.key(seed), 16)
    return {
        "tokens": normal_values(streams_of[0], (TOKENS, D), 1.0, 6.0, ((0, 8),)),
        "codebook": normal_values(streams_of[1], (CODES, D), 1.0, 6.0),
        "codes": place_ends(jax.random.randint(streams_of[2], (TOKENS,), 0, CODES), jax.random.fold_in(streams_of[2], 1), 0, CODES - 1).astype(jnp.int32),
        "modality": draw_modality(jax.random.fold_in(streams_of[15], 71), 0),
        "segments": jax.vmap(lambda own: jnp.searchsorted(jnp.cumsum(ragged_sizes(own, 8, TOK_DEV, TOK_DEV // 2, 1)), jnp.arange(TOK_DEV), side="right"))(jax.random.split(streams_of[4], N_SEQ)).reshape((N_SEQ, TOK_DEV)).astype(jnp.int32),
        "sequence_source": draw_sequence_source(jax.random.fold_in(streams_of[15], 71), 0),
        "w_qkv": normal_values(streams_of[6], (D, 3, D), D ** -0.5, 0.125, ((2, 4),)),
        "w_out": normal_values(streams_of[7], (D, D), (max(D // 64, 1)) ** -0.5, 1.0, ((0, 4),)),
        "w_up": normal_values(streams_of[8], (D, FF), D ** -0.5, 0.125, ((1, 4),)),
        "w_down": normal_values(streams_of[9], (FF, D), FF ** -0.5, 0.0625, ((0, 4),)),
        "norm1_gain": jnp.clip(1.0 + 0.18 * jax.random.normal(streams_of[10], (D,), jnp.float32), 0.1, 1.9),
        "norm1_shift": normal_values(streams_of[11], (D,), 0.3, 4.0, (), jnp.float32),
        "norm2_gain": jnp.clip(1.0 + 0.18 * jax.random.normal(streams_of[12], (D,), jnp.float32), 0.1, 1.9),
        "norm2_shift": normal_values(streams_of[13], (D,), 0.3, 4.0, (), jnp.float32),
        "cotangent": gaussian_with(streams_of[14], (TOKENS, D), 1.0, 6.0, ((0, 8),), (0, 1, 8, 2.0)),
    }


@jax.custom_vjp
def low(v):
    return lax.optimization_barrier(v.astype(jnp.bfloat16)).astype(jnp.float32)

@jax.custom_vjp
def low_back(v):
    return v

def low_keep(v):
    return (low(v), None)

def low_pass(kept, grad):
    return (grad,)

def back_keep(v):
    return (v, None)

def back_low(kept, grad):
    return (low(grad),)
low.defvjp(low_keep, low_pass)
low_back.defvjp(back_keep, back_low)

def layer_norm(values, gain, shift):
    centre = values - lax.optimization_barrier(jnp.mean(values, axis=-1, keepdims=True))
    variance = lax.optimization_barrier(jnp.mean(centre * centre, axis=-1, keepdims=True))
    return centre * lax.rsqrt(variance + 1e-05) * gain + shift

def reference(tokens, codebook, codes, modality, segments, sequence_source, w_qkv, w_out, w_up, w_down, norm1_gain, norm1_shift, norm2_gain, norm2_shift, cotangent):
    highest = lax.Precision.HIGHEST
    image = (modality == 1).astype(jnp.float32)[:, None]
    looked = jnp.take(codebook.astype(jnp.float32), codes, axis=0) * image
    back_index = jnp.argsort(sequence_source).astype(jnp.int32)
    positions = jnp.arange(TOK_DEV, dtype=jnp.int32)
    causal = positions[None, :] <= positions[:, None]
    factor = 1.0 / math.sqrt(HEAD_DIM)

    def attend(block):
        row_qkv, segment_row = block
        queries = row_qkv[:, 0]
        keys_part = row_qkv[:, 1]
        values_part = row_qkv[:, 2]
        scores = low_back(jnp.einsum('qhc,khc->hqk', queries, keys_part, precision=highest) * factor)
        allowed = (segment_row[:, None] == segment_row[None, :]) & causal
        scores = jnp.where(allowed[None], scores, -1e+30)
        probs = low(jax.nn.softmax(scores, axis=-1))
        return jnp.einsum('hqk,khc->qhc', probs, values_part, precision=highest).reshape(TOK_DEV, D)

    def layer(inputs, qkv_weight, out_weight, up_weight, down_weight, gain_one, shift_one, gain_two, shift_two):
        embedded = inputs + looked
        normed_one = low(layer_norm(embedded, gain_one, shift_one))
        qkv = low_back(low(jnp.einsum('td,dsc->tsc', normed_one, qkv_weight, precision=highest)))
        ordered = qkv[sequence_source].reshape(N_SEQ, TOK_DEV, 3, HEADS, HEAD_DIM)
        mixed = lax.map(jax.checkpoint(attend), (ordered, segments)).reshape(TOKENS, D)
        context = low_back(low(mixed))[back_index]
        attended = low_back(jnp.dot(context, out_weight, precision=highest))
        hidden_in = embedded + attended
        normed_two = low(layer_norm(hidden_in, gain_two, shift_two))
        up_value = low_back(jnp.dot(normed_two, up_weight, precision=highest))
        act_low = low(jax.nn.gelu(up_value, approximate=False))
        return hidden_in + jnp.dot(act_low, down_weight, precision=highest)
    output, pull = jax.vjp(layer, tokens.astype(jnp.float32), w_qkv.astype(jnp.float32), w_out.astype(jnp.float32), w_up.astype(jnp.float32), w_down.astype(jnp.float32), norm1_gain, norm1_shift, norm2_gain, norm2_shift)
    grads = pull(cotangent.astype(jnp.float32))
    return (output.astype(jnp.bfloat16), grads[0].astype(jnp.bfloat16), grads[1], grads[2], grads[3], grads[4], grads[5], grads[6], grads[7], grads[8])
```

```python
from functools import partial
import math

import jax
import jax.numpy as jnp
from jax import lax
from jax.experimental import pallas as pl
from jax.experimental.pallas import tpu as pltpu
from jax.sharding import PartitionSpec as P

HEAD_DIM = 128
F32 = jnp.float32
BF16 = jnp.bfloat16
MIB = 1 << 20


def params(limit=40):
    return pltpu.CompilerParams(vmem_limit_bytes=limit * MIB)


def cost(flops, moved, special=0):
    return pl.CostEstimate(flops=int(flops), bytes_accessed=int(moved), transcendentals=int(special))


def dot(a, b, contract=((1,), (0,))):
    return lax.dot_general(a, b, (contract, ((), ())), preferred_element_type=F32)


NT = ((1,), (1,))
TN = ((0,), (0,))


def matmul(a, b, transposed=False, start=0, rows=None, tile_m=512, tile_n=512, out=BF16):
    rows = rows or a.shape[0]
    depth = a.shape[1]
    width = b.shape[0] if transposed else b.shape[1]
    tile_m, tile_n = min(tile_m, rows), min(tile_n, width)
    first = start // tile_m

    def body(a_ref, b_ref, o_ref):
        o_ref[...] = dot(a_ref[...], b_ref[...], NT if transposed else ((1,), (0,))).astype(out)

    return pl.pallas_call(
        body,
        grid=(rows // tile_m, width // tile_n),
        in_specs=[
            pl.BlockSpec((tile_m, depth), lambda i, j: (i + first, 0)),
            pl.BlockSpec((tile_n, depth), lambda i, j: (j, 0))
            if transposed
            else pl.BlockSpec((depth, tile_n), lambda i, j: (0, j)),
        ],
        out_specs=pl.BlockSpec((tile_m, tile_n), lambda i, j: (i, j)),
        out_shape=jax.ShapeDtypeStruct((rows, width), out),
        compiler_params=params(),
        cost_estimate=cost(2 * rows * width * depth, 2 * (rows * depth + width * depth + rows * width)),
    )(a, b)


def project(a, w3):
    rows, depth = a.shape
    width = w3.shape[2]

    def body(a_ref, w_ref, o_ref):
        o_ref[0] = dot(a_ref[...], w_ref[0]).astype(BF16)

    return pl.pallas_call(
        body,
        grid=(3,),
        in_specs=[
            pl.BlockSpec((rows, depth), lambda s: (0, 0)),
            pl.BlockSpec((1, depth, width), lambda s: (s, 0, 0)),
        ],
        out_specs=pl.BlockSpec((1, rows, width), lambda s: (s, 0, 0)),
        out_shape=jax.ShapeDtypeStruct((3, rows, width), BF16),
        compiler_params=params(),
        cost_estimate=cost(6 * rows * width * depth, 2 * (rows * depth + 3 * width * (depth + rows))),
    )(a, w3)


def project_back(g3, w3, start, rows, tile_n=512):
    width, depth = g3.shape[2], w3.shape[1]
    first = start // rows

    def body(g_ref, w_ref, o_ref):
        total = dot(g_ref[0], w_ref[0], NT)
        total += dot(g_ref[1], w_ref[1], NT)
        total += dot(g_ref[2], w_ref[2], NT)
        o_ref[...] = total.astype(BF16)

    return pl.pallas_call(
        body,
        grid=(depth // tile_n,),
        in_specs=[
            pl.BlockSpec((3, rows, width), lambda j: (0, first, 0)),
            pl.BlockSpec((3, tile_n, width), lambda j: (0, j, 0)),
        ],
        out_specs=pl.BlockSpec((rows, tile_n), lambda j: (0, j)),
        out_shape=jax.ShapeDtypeStruct((rows, depth), BF16),
        compiler_params=params(),
        cost_estimate=cost(6 * rows * width * depth, 2 * (rows * depth + 3 * width * (depth + rows))),
    )(g3, w3)


def mlp(normed, cot, w_up, w_down, tile=256):
    rows, depth = normed.shape
    width = w_up.shape[1]

    def body(n_ref, c_ref, u_ref, d_ref, act_ref, bar_ref):
        up = dot(n_ref[...], u_ref[...])
        grad = dot(c_ref[...], d_ref[...], NT)
        bell = jnp.exp(up * up * -0.5)
        t = 1.0 / (1.0 + (0.3275911 / math.sqrt(2.0)) * jnp.abs(up))
        poly = t * (
            0.127414796 + t * (-0.142248368 + t * (0.7107068705 + t * (-0.7265760135 + t * 0.5307027145)))
        )
        tail = poly * bell
        phi = jnp.where(up < 0.0, tail, 1.0 - tail)
        act_ref[...] = (up * phi).astype(BF16)
        slope = phi + up * bell * (1.0 / math.sqrt(2.0 * math.pi))
        bar_ref[...] = (slope * grad).astype(BF16)

    return pl.pallas_call(
        body,
        grid=(width // tile,),
        in_specs=[
            pl.BlockSpec((rows, depth), lambda j: (0, 0)),
            pl.BlockSpec((rows, depth), lambda j: (0, 0)),
            pl.BlockSpec((depth, tile), lambda j: (0, j)),
            pl.BlockSpec((tile, depth), lambda j: (j, 0)),
        ],
        out_specs=[pl.BlockSpec((rows, tile), lambda j: (0, j))] * 2,
        out_shape=[jax.ShapeDtypeStruct((rows, width), BF16)] * 2,
        compiler_params=params(),
        cost_estimate=cost(
            4 * rows * width * depth, 4 * (rows * depth + depth * width + rows * width), rows * width
        ),
    )(normed, cot, w_up, w_down)


def attend(qkv, pos_col, start_col, pos_row, tile=256):
    _, rows, width = qkv.shape
    heads = width // HEAD_DIM
    factor = 1.0 / math.sqrt(HEAD_DIM)

    def body(q_ref, kv_ref, pc_ref, sc_ref, pr_ref, o_ref):
        keys = pr_ref[...]
        seen = (keys <= pc_ref[...]) & (keys >= sc_ref[...])
        bias = jnp.where(seen, 0.0, -1e30)
        for head in range(heads):
            cols = slice(head * HEAD_DIM, (head + 1) * HEAD_DIM)
            scores = dot(q_ref[0, :, cols], kv_ref[1, :, cols], NT) * factor + bias
            peak = jnp.max(scores, axis=-1, keepdims=True)
            grown = jnp.exp(scores - peak)
            total = jnp.sum(grown, axis=-1, keepdims=True)
            probs = (grown * (1.0 / total)).astype(BF16)
            o_ref[:, cols] = dot(probs, kv_ref[2, :, cols]).astype(BF16)

    return pl.pallas_call(
        body,
        grid=(rows // tile,),
        in_specs=[
            pl.BlockSpec((1, tile, width), lambda i: (0, i, 0)),
            pl.BlockSpec((3, rows, width), lambda i: (0, 0, 0)),
            pl.BlockSpec((tile, 1), lambda i: (i, 0)),
            pl.BlockSpec((tile, 1), lambda i: (i, 0)),
            pl.BlockSpec((1, rows), lambda i: (0, 0)),
        ],
        out_specs=pl.BlockSpec((tile, width), lambda i: (i, 0)),
        out_shape=jax.ShapeDtypeStruct((rows, width), BF16),
        compiler_params=params(),
        cost_estimate=cost(8 * rows * rows * width, 10 * rows * width, heads * rows * rows),
    )(qkv, qkv, pos_col, start_col, pos_row)


def attend_back(qkv, bar, pos_col, pos_row, start_row, tile=256):
    _, rows, width = qkv.shape
    heads = width // HEAD_DIM
    factor = 1.0 / math.sqrt(HEAD_DIM)

    def body(q_ref, kv_ref, g_ref, pc_ref, pr_ref, sr_ref, o_ref, dk, dv):
        step = pl.program_id(0)
        keys = pc_ref[...]
        seen = (keys <= pr_ref[...]) & (keys >= sr_ref[...])
        bias = jnp.where(seen, 0.0, -1e30)

        @pl.when(step == 0)
        def _():
            dk[...] = jnp.zeros_like(dk)
            dv[...] = jnp.zeros_like(dv)

        for head in range(heads):
            cols = slice(head * HEAD_DIM, (head + 1) * HEAD_DIM)
            q, k, v, g = q_ref[0, :, cols], kv_ref[1, :, cols], kv_ref[2, :, cols], g_ref[:, cols]
            scores = dot(k, q, NT) * factor + bias
            peak = jnp.max(scores, axis=0, keepdims=True)
            grown = jnp.exp(scores - peak)
            probs = grown * (1.0 / jnp.sum(grown, axis=0, keepdims=True))
            dv[:, cols] += dot(probs.astype(BF16), g)
            probs_bar = dot(v, g, NT)
            inner = jnp.sum(probs * probs_bar, axis=0, keepdims=True)
            scores_bar = (probs * (probs_bar - inner)).astype(BF16)
            dk[:, cols] += dot(scores_bar, q)
            dq = dot(scores_bar, k, TN) * factor
            o_ref[0, pl.ds(pl.multiple_of(step * tile, tile), tile), cols] = dq.astype(BF16)

        @pl.when(step == pl.num_programs(0) - 1)
        def _():
            o_ref[1] = (dk[...] * factor).astype(BF16)
            o_ref[2] = dv[...].astype(BF16)

    return pl.pallas_call(
        body,
        grid=(rows // tile,),
        in_specs=[
            pl.BlockSpec((1, tile, width), lambda i: (0, i, 0)),
            pl.BlockSpec((3, rows, width), lambda i: (0, 0, 0)),
            pl.BlockSpec((tile, width), lambda i: (i, 0)),
            pl.BlockSpec((rows, 1), lambda i: (0, 0)),
            pl.BlockSpec((1, tile), lambda i: (0, i)),
            pl.BlockSpec((1, tile), lambda i: (0, i)),
        ],
        out_specs=pl.BlockSpec((3, rows, width), lambda i: (0, 0, 0)),
        out_shape=jax.ShapeDtypeStruct((3, rows, width), BF16),
        scratch_shapes=[pltpu.VMEM((rows, width), F32)] * 2,
        compiler_params=params(),
        cost_estimate=cost(16 * rows * rows * width, 16 * rows * width, heads * rows * rows),
    )(qkv, qkv, bar, pos_col, pos_row, start_row)


def weight_grad(ids, left, right, received=None):
    count = ids.shape[0]
    rows, depth = left.shape
    block = depth // (2 * count)
    if block % 128:
        picked = jnp.take(left.reshape(rows, 2 * count, block), ids, axis=1).reshape(rows, depth // 2)
        wide = depth // 256
        padded = jnp.concatenate([picked, picked], axis=1)
        if received is not None:
            received = received.reshape(wide, 128, -1)
        result = weight_grad(jnp.arange(wide, dtype=jnp.int32), padded, right, received)
        return result.reshape(count, block, -1)
    if right.ndim == 2:
        right = right[None]
    parts, _, width = right.shape

    def body(ids_ref, l_ref, r_ref, *rest):
        o_ref = rest[-1]
        for part in range(parts):
            cols = slice(part * width, (part + 1) * width)
            total = dot(l_ref[...], r_ref[part], TN)
            if received is not None:
                total += rest[0][0, :, cols].astype(F32)
            o_ref[0, :, cols] = total.astype(BF16)

    specs = [
        pl.BlockSpec((rows, block), lambda j, ids: (0, ids[j])),
        pl.BlockSpec((parts, rows, width), lambda j, ids: (0, 0, 0)),
    ]
    result = pl.BlockSpec((1, block, parts * width), lambda j, ids: (j, 0, 0))
    more = []
    if received is not None:
        specs.append(result)
        more.append(received)
    return pl.pallas_call(
        body,
        grid_spec=pltpu.PrefetchScalarGridSpec(
            num_scalar_prefetch=1, grid=(count,), in_specs=specs, out_specs=result
        ),
        out_shape=jax.ShapeDtypeStruct((count, block, parts * width), BF16),
        compiler_params=params(),
        cost_estimate=cost(
            rows * depth * parts * width, rows * depth + 2 * rows * parts * width + 2 * depth * parts * width
        ),
    )(ids, left, right, *more)


def normalize(values):
    centre = values - jnp.mean(values, axis=-1, keepdims=True)
    scaling = lax.rsqrt(jnp.mean(centre * centre, axis=-1, keepdims=True) + 1e-05)
    return (centre * scaling, scaling)


def norm_back(upstream, unit, scaling, gain):
    scaled = upstream * gain
    inner = (
        scaled
        - jnp.mean(scaled, axis=-1, keepdims=True)
        - unit * jnp.mean(scaled * unit, axis=-1, keepdims=True)
    )
    return (scaling * inner, jnp.sum(upstream * unit, axis=0), jnp.sum(upstream, axis=0))


def local(
    n_seq,
    n_head,
    tokens,
    codebook,
    codes,
    modality,
    segments,
    sequence_source,
    w_qkv,
    w_out,
    w_up,
    w_down,
    norm1_gain,
    norm1_shift,
    norm2_gain,
    norm2_shift,
    cotangent,
):
    rows, depth = tokens.shape
    me, own = lax.axis_index("seq"), lax.axis_index("head")
    share = rows // n_seq // n_head
    slice_rows = rows // n_head
    half = rows // 2
    w3 = jnp.transpose(w_qkv, (1, 0, 2))

    def swap(x, flip, axis="head"):
        size = n_head if axis == "head" else n_seq
        return lax.ppermute(x, axis, [(i, i ^ flip) for i in range(size)])

    def gather(x):
        core, across = swap(x, 1), swap(x, 2)
        return jnp.concatenate([x, core], axis=0), jnp.concatenate([across, swap(across, 1)], axis=0)

    def scatter_sum(high, low):
        passed = high[:slice_rows].astype(F32) + swap(high[slice_rows:], 1).astype(F32)
        across = swap(passed.astype(BF16), 2)
        near = low[:slice_rows].astype(F32) + swap(low[slice_rows:], 1).astype(F32)
        return near + across.astype(F32)

    def exchange(x):
        return lax.all_to_all(x, "seq", split_axis=0, concat_axis=0, tiled=True)

    source = sequence_source.reshape(n_seq, rows)
    places = jnp.arange(rows, dtype=jnp.int32)
    groups = source // rows
    offsets = source % rows
    leaving = groups == me
    coming = lax.dynamic_index_in_dim(groups, me, 0) == jnp.arange(n_seq, dtype=jnp.int32)[:, None]
    upper = (places[:, None] <= places[None, :]).astype(BF16)
    counts = jnp.dot(
        jnp.concatenate([leaving, coming], axis=0).astype(BF16), upper, preferred_element_type=F32
    ).astype(jnp.int32)
    leaving_rank = jnp.where(leaving, counts[:n_seq] - 1, -1)
    coming_rank = jnp.where(coming, counts[n_seq:] - 1, -1)
    lanes = jnp.arange(share, dtype=jnp.int32)

    def listed(rank, value, blocks):
        wanted = (own ^ jnp.asarray(blocks, jnp.int32))[:, None] * share + lanes[None, :]
        hit = rank[None, :, None, :] == wanted[:, None, :, None]
        return jnp.sum(jnp.where(hit, value[None, :, None, :], 0), axis=-1).reshape(-1)

    sent = listed(leaving_rank, offsets, [0])
    pick = (sent[:, None] == places[None, :]).astype(BF16)
    code = jnp.where(modality == 1, codes, -1)
    sent_code = jnp.sum(jnp.where(sent[:, None] == places[None, :], code[None, :], 0), axis=-1)
    pick_code = (
        sent_code[:, None] == jnp.arange(codebook.shape[0], dtype=jnp.int32)[None, :]
    ).astype(BF16)
    leaving_embedded = (
        jnp.dot(pick, tokens, preferred_element_type=F32)
        + jnp.dot(pick_code, codebook, preferred_element_type=F32)
    ).astype(BF16)
    leaving_cot = jnp.dot(pick, cotangent, preferred_element_type=F32).astype(BF16)

    embedded = exchange(leaving_embedded).astype(F32)
    cot_slice = exchange(leaving_cot)

    every = list(range(n_head))
    sent_all = listed(leaving_rank, offsets, every)
    segment_row = segments[0]
    begin = jnp.sum((segment_row[:, None] < segment_row[None, :]).astype(jnp.int32), axis=0)
    packed = listed(coming_rank, jnp.broadcast_to(begin * rows + places, (n_seq, rows)), every)
    position, start = packed % rows, packed // rows
    back = (places[:, None] == sent_all[None, :]).astype(BF16)

    unit_one, scale_one = normalize(embedded)
    normed_one = jnp.concatenate(gather((unit_one * norm1_gain + norm1_shift).astype(BF16)), axis=0)
    qkv = project(normed_one, w3)
    mixed = attend(qkv, position[:, None], start[:, None], position[None, :])
    attended = scatter_sum(
        matmul(mixed, w_out, start=half, rows=half), matmul(mixed, w_out, start=0, rows=half)
    )
    hidden_in = embedded + attended
    unit_two, scale_two = normalize(hidden_in)
    normed_low, normed_high = gather((unit_two * norm2_gain + norm2_shift).astype(BF16))
    cot_low, cot_high = gather(cot_slice)
    act_low, bar_low = mlp(normed_low, cot_low, w_up, w_down)
    act_high, bar_high = mlp(normed_high, cot_high, w_up, w_down)

    normed_two_bar = scatter_sum(
        matmul(bar_high, w_up, transposed=True), matmul(bar_low, w_up, transposed=True)
    )
    normed_two = jnp.concatenate([normed_low, normed_high], axis=0)
    cot_all = jnp.concatenate([cot_low, cot_high], axis=0)
    act = jnp.concatenate([act_low, act_high], axis=0)
    up_bar = jnp.concatenate([bar_low, bar_high], axis=0)

    steps = 2 * jnp.arange(n_seq // 2, dtype=jnp.int32)
    mine, others = me ^ steps, me ^ 1 ^ steps

    def reduce_grad(left, right):
        passed = swap(weight_grad(others, left, right), 1, "seq")
        mine_sum = weight_grad(mine, left, right, passed)
        total = mine_sum[0].astype(F32)
        for j in range(1, n_seq // 2):
            total = total + swap(mine_sum[j], 2 * j, "seq").astype(F32)
        return total

    down_grad = reduce_grad(cot_all, act).T
    up_grad = reduce_grad(normed_two, up_bar)

    branch = scatter_sum(matmul(act_high, w_down), matmul(act_low, w_down))
    output_slice = (hidden_in + branch).astype(BF16)

    def send_home(x):
        return jnp.dot(
            back, jnp.concatenate(gather(exchange(x)), axis=0), preferred_element_type=F32
        ).astype(BF16)

    block_output = send_home(output_slice)

    hidden_part, gain_two, shift_two = norm_back(normed_two_bar, unit_two, scale_two, norm2_gain)
    hidden_bar = cot_slice.astype(F32) + hidden_part
    hidden_low = jnp.concatenate(gather(hidden_bar.astype(BF16)), axis=0)
    context_bar = matmul(hidden_low, w_out, transposed=True)
    out_grad = reduce_grad(hidden_low, mixed).T
    qkv_bar = attend_back(qkv, context_bar, position[:, None], position[None, :], start[None, :])
    normed_one_bar = scatter_sum(
        project_back(qkv_bar, w3, half, half), project_back(qkv_bar, w3, 0, half)
    )
    qkv_grad = reduce_grad(normed_one, qkv_bar)
    qkv_grad = jnp.transpose(qkv_grad.reshape(depth // n_seq, 3, -1), (0, 1, 2))
    input_part, gain_one, shift_one = norm_back(normed_one_bar, unit_one, scale_one, norm1_gain)
    input_grad = send_home((hidden_bar + input_part).astype(BF16))

    vectors = jnp.stack([gain_one, shift_one, gain_two, shift_two])
    vectors = vectors + swap(vectors, 1)
    vectors = vectors + swap(vectors, 2)
    vectors = jnp.transpose(vectors.reshape(4, n_seq, depth // n_seq), (1, 0, 2))
    vectors = jnp.sum(exchange(vectors), axis=0)
    return (
        block_output,
        input_grad,
        qkv_grad,
        out_grad,
        up_grad,
        down_grad,
        vectors[0],
        vectors[1],
        vectors[2],
        vectors[3],
    )


def solution(mesh):
    return jax.shard_map(
        partial(local, mesh.shape["seq"], mesh.shape["head"]),
        mesh=mesh,
        in_specs=(
            P("seq", None),
            P(),
            P("seq"),
            P("seq"),
            P("seq", None),
            P(),
            P(None, None, "head"),
            P("head", None),
            P(None, "head"),
            P("head", None),
            P(),
            P(),
            P(),
            P(),
            P("seq", None),
        ),
        out_specs=(
            P("seq", None),
            P("seq", None),
            P("seq", None, "head"),
            P("head", "seq"),
            P("seq", "head"),
            P("head", "seq"),
            P("seq"),
            P("seq"),
            P("seq"),
            P("seq"),
        ),
        check_vma=False,
    )
```

```python
from functools import partial
import math

import jax
import jax.numpy as jnp
from jax import lax
from jax.experimental import pallas as pl
from jax.experimental.pallas import tpu as pltpu
from jax.sharding import PartitionSpec as P

HEAD_DIM = 128
F32 = jnp.float32
BF16 = jnp.bfloat16
MIB = 1 << 20
NN = ((1,), (0,))
NT = ((1,), (1,))
TN = ((0,), (0,))


def dot(a, b, contract=NN):
    return lax.dot_general(a, b, (contract, ((), ())), preferred_element_type=F32)


def call(body, grid, ins, outs, scratch=(), flops=0, special=0, after=(), prefetch=None):
    arrays = [array for array, _, _ in ins]
    specs = [pl.BlockSpec(block, index) for _, block, index in ins] + [pl.BlockSpec(memory_space=pl.ANY)] * len(after)
    shapes = [jax.ShapeDtypeStruct(shape, kind) for shape, kind, _, _ in outs]
    n_in, n_pre = len(ins), 0 if prefetch is None else 1

    def wrapped(*refs):
        body(*refs[: n_pre + n_in], *refs[n_pre + n_in + len(after) :])

    moved = sum(a.size * a.dtype.itemsize for a in arrays) + sum(s.size * s.dtype.itemsize for s in shapes)
    out_specs = [pl.BlockSpec(block, index) for _, _, block, index in outs]
    keys = dict(
        out_shape=shapes,
        compiler_params=pltpu.CompilerParams(vmem_limit_bytes=55 * MIB),
        cost_estimate=pl.CostEstimate(flops=0, bytes_accessed=0, transcendentals=0),
    )
    if prefetch is None:
        made = pl.pallas_call(
            wrapped, grid=grid, in_specs=specs, out_specs=out_specs, scratch_shapes=list(scratch), **keys
        )
        return made(*arrays, *after)
    spec = pltpu.PrefetchScalarGridSpec(
        num_scalar_prefetch=1, grid=grid, in_specs=specs, out_specs=out_specs, scratch_shapes=list(scratch)
    )
    return pl.pallas_call(wrapped, grid_spec=spec, **keys)(prefetch, *arrays, *after)


def gate(x, *after):
    def body(*refs):
        pass

    anywhere = pl.BlockSpec(memory_space=pl.ANY)
    return pl.pallas_call(
        body,
        in_specs=[anywhere] * (1 + len(after)),
        out_specs=anywhere,
        out_shape=jax.ShapeDtypeStruct(x.shape, x.dtype),
        input_output_aliases={0: 0},
        cost_estimate=pl.CostEstimate(flops=0, bytes_accessed=0, transcendentals=0),
    )(x, *after)


def block_matmul(picks, b, transposed=False, tile=512, received=None, after=()):
    rows, depth = picks[0][0].shape[0] // picks[0][2], picks[0][0].shape[1]
    width = b.shape[0] if transposed else b.shape[1]

    def body(x_ref, y_ref, b_ref, *rest):
        o_ref, p_ref, both = rest[-3:]

        @pl.when(pl.program_id(0) == 0)
        def _():
            both[:rows] = x_ref[...]
            both[rows:] = y_ref[...]

        result = dot(both[...], b_ref[...], NT if transposed else NN)
        o_ref[...] = result[:rows].astype(BF16)
        second = result[rows:]
        if received is not None:
            second += rest[0][...].astype(F32)
        p_ref[...] = second.astype(BF16)

    side = ((tile, depth), lambda j: (j, 0)) if transposed else ((depth, tile), lambda j: (0, j))
    more = [] if received is None else [(received, (rows, tile), lambda j: (0, j))]
    return call(
        body,
        (width // tile,),
        [(x, (rows, depth), lambda j, n=n: (n, 0)) for x, n, _ in picks] + [(b, *side)] + more,
        [((rows, width), BF16, (rows, tile), lambda j: (0, j))] * 2,
        [pltpu.VMEM((2 * rows, depth), BF16)],
        flops=4 * rows * width * depth,
        after=after,
    )


def project(pair, w3, after=()):
    rows, depth = pair[0].shape
    width = w3.shape[2]

    def body(x_ref, y_ref, w_ref, o_ref, both):
        @pl.when(pl.program_id(0) == 0)
        def _():
            both[:rows] = x_ref[...]
            both[rows:] = y_ref[...]

        o_ref[0] = dot(both[...], w_ref[0]).astype(BF16)

    return call(
        body,
        (3,),
        [(x, (rows, depth), lambda s: (0, 0)) for x in pair]
        + [(w3, (1, depth, width), lambda s: (s, 0, 0))],
        [((3, 2 * rows, width), BF16, (1, 2 * rows, width), lambda s: (s, 0, 0))],
        [pltpu.VMEM((2 * rows, depth), BF16)],
        flops=12 * rows * width * depth,
        after=after,
    )[0]


def project_back(g3, w3, picks, tile=512, received=None, after=()):
    width, depth, rows = g3.shape[2], w3.shape[1], g3.shape[1] // 4

    def body(x_ref, y_ref, w_ref, *rest):
        o_ref, p_ref, both = rest[-3:]

        @pl.when(pl.program_id(0) == 0)
        def _():
            both[:, :rows] = x_ref[...]
            both[:, rows:] = y_ref[...]

        total = dot(both[0], w_ref[0], NT)
        total += dot(both[1], w_ref[1], NT)
        total += dot(both[2], w_ref[2], NT)
        o_ref[...] = total[:rows].astype(BF16)
        second = total[rows:]
        if received is not None:
            second += rest[0][...].astype(F32)
        p_ref[...] = second.astype(BF16)

    more = [] if received is None else [(received, (rows, tile), lambda j: (0, j))]
    return call(
        body,
        (depth // tile,),
        [(g3, (3, rows, width), lambda j, n=n: (0, n, 0)) for n in picks]
        + [(w3, (3, tile, width), lambda j: (0, j, 0))]
        + more,
        [((rows, depth), BF16, (rows, tile), lambda j: (0, j))] * 2,
        [pltpu.VMEM((3, 2 * rows, width), BF16)],
        flops=12 * rows * width * depth,
        after=after,
    )


def mlp(normed, cot, w_up, w_down, tile=512, after=()):
    rows, depth = normed[0].shape
    width = w_up.shape[1]

    def body(n0, n1, c0, c1, u_ref, d_ref, act_ref, bar_ref, n_both, c_both):
        @pl.when(pl.program_id(0) == 0)
        def _():
            n_both[:rows] = n0[...]
            n_both[rows:] = n1[...]
            c_both[:rows] = c0[...]
            c_both[rows:] = c1[...]

        up = dot(n_both[...], u_ref[...])
        grad = dot(c_both[...], d_ref[...], NT)
        bell = jnp.exp(up * up * -0.5)
        t = 1.0 / (1.0 + (0.3275911 / math.sqrt(2.0)) * jnp.abs(up))
        poly = t * (
            0.127414796 + t * (-0.142248368 + t * (0.7107068705 + t * (-0.7265760135 + t * 0.5307027145)))
        )
        tail = poly * bell
        phi = jnp.where(up < 0.0, tail, 1.0 - tail)
        act_ref[...] = (up * phi).astype(BF16)
        slope = phi + up * bell * (1.0 / math.sqrt(2.0 * math.pi))
        bar_ref[...] = (slope * grad).astype(BF16)

    return call(
        body,
        (width // tile,),
        [(x, (rows, depth), lambda j: (0, 0)) for x in (*normed, *cot)]
        + [(w_up, (depth, tile), lambda j: (0, j)), (w_down, (tile, depth), lambda j: (j, 0))],
        [((2 * rows, width), BF16, (2 * rows, tile), lambda j: (0, j))] * 2,
        [pltpu.VMEM((2 * rows, depth), BF16)] * 2,
        flops=8 * rows * width * depth,
        special=4 * rows * width,
        after=after,
    )


def attend(picks, qkv, pos_col, start_col, pos_row, after=()):
    _, half, width = qkv[0].shape
    rows = half // 2
    heads = width // HEAD_DIM
    factor = 1.0 / math.sqrt(HEAD_DIM)

    def body(x_ref, y_ref, low_ref, high_ref, px_ref, py_ref, sx_ref, sy_ref, pr_ref, o_ref, kv, both):
        i = pl.program_id(0)

        @pl.when(i == 0)
        def _():
            kv[:, :half] = low_ref[1:]
            kv[:, half:] = high_ref[1:]
            both[0] = x_ref[0]
            both[1] = y_ref[0]

        keys = pr_ref[...]
        at = jnp.where(i == 0, px_ref[...], py_ref[...])
        since = jnp.where(i == 0, sx_ref[...], sy_ref[...])
        bias = jnp.where((keys <= at) & (keys >= since), 0.0, -1e30)
        for head in range(heads):
            cols = slice(head * HEAD_DIM, (head + 1) * HEAD_DIM)
            scores = dot(both[i, :, cols], kv[0, :, cols], NT) * factor + bias
            peak = jnp.max(scores, axis=-1, keepdims=True)
            grown = jnp.exp(scores - peak)
            total = jnp.sum(grown, axis=-1, keepdims=True)
            o_ref[:, cols] = (dot(grown.astype(BF16), kv[1, :, cols]) * (1.0 / total)).astype(BF16)

    return call(
        body,
        (2,),
        [(qkv[n // 2], (1, rows, width), lambda i, n=n: (0, n % 2, 0)) for n in picks]
        + [
            (qkv[0], (3, half, width), lambda i: (0, 0, 0)),
            (qkv[1], (3, half, width), lambda i: (0, 0, 0)),
        ]
        + [(c, (rows, 1), lambda i, n=n: (n, 0)) for c in (pos_col, start_col) for n in picks]
        + [(pos_row, (1, 2 * half), lambda i: (0, 0))],
        [((half, width), BF16, (rows, width), lambda i: (i, 0))],
        [pltpu.VMEM((2, 2 * half, width), BF16), pltpu.VMEM((2, rows, width), BF16)],
        flops=8 * half * half * width,
        special=2 * heads * half * half,
        after=after,
    )[0]


def attend_back(qkv, bars, pos_col, pos_row, start_row, after=()):
    _, half, width = qkv[0].shape
    rows = 2 * half
    tile = rows // 4
    heads = width // HEAD_DIM
    factor = 1.0 / math.sqrt(HEAD_DIM)

    def body(low_ref, high_ref, g0, g1, g2, g3, pc_ref, pr_ref, sr_ref, o_ref, all_qkv, dk, dv, g_tile):
        step = pl.program_id(0)
        keys = pc_ref[...]
        seen = (keys <= pr_ref[...]) & (keys >= sr_ref[...])
        bias = jnp.where(seen, 0.0, -1e30)

        @pl.when(step == 0)
        def _():
            dk[...] = jnp.zeros_like(dk)
            dv[...] = jnp.zeros_like(dv)
            all_qkv[:, :half] = low_ref[...]
            all_qkv[:, half:] = high_ref[...]

        for number, g_ref in enumerate((g0, g1, g2, g3)):

            @pl.when(step == number)
            def _():
                g_tile[...] = g_ref[...]

        here = pl.ds(pl.multiple_of(step * tile, tile), tile)
        for head in range(heads):
            cols = slice(head * HEAD_DIM, (head + 1) * HEAD_DIM)
            q, k, v, g = all_qkv[0, here, cols], all_qkv[1, :, cols], all_qkv[2, :, cols], g_tile[:, cols]
            scores = dot(k, q, NT) * factor + bias
            peak = jnp.max(scores, axis=0, keepdims=True)
            grown = jnp.exp(scores - peak)
            probs = grown * (1.0 / jnp.sum(grown, axis=0, keepdims=True))
            dv[:, cols] += dot(probs.astype(BF16), g)
            probs_bar = dot(v, g, NT)
            inner = jnp.sum(probs * probs_bar, axis=0, keepdims=True)
            scores_bar = (probs * (probs_bar - inner)).astype(BF16)
            dk[:, cols] += dot(scores_bar, q)
            dq = dot(scores_bar, k, TN) * factor
            o_ref[0, here, cols] = dq.astype(BF16)

        @pl.when(step == pl.num_programs(0) - 1)
        def _():
            o_ref[1] = (dk[...] * factor).astype(BF16)
            o_ref[2] = dv[...].astype(BF16)

    return call(
        body,
        (4,),
        [
            (qkv[0], (3, half, width), lambda i: (0, 0, 0)),
            (qkv[1], (3, half, width), lambda i: (0, 0, 0)),
            *[(bar, (tile, width), lambda i: (0, 0)) for bar in bars],
            (pos_col, (rows, 1), lambda i: (0, 0)),
            (pos_row, (1, tile), lambda i: (0, i)),
            (start_row, (1, tile), lambda i: (0, i)),
        ],
        [((3, rows, width), BF16, (3, rows, width), lambda i: (0, 0, 0))],
        [
            pltpu.VMEM((3, rows, width), BF16),
            pltpu.VMEM((rows, width), F32),
            pltpu.VMEM((rows, width), F32),
            pltpu.VMEM((tile, width), BF16),
        ],
        flops=10 * rows * rows * width,
        special=heads * rows * rows,
        after=after,
    )[0]


def weight_grad(ids, lefts, rights, piece, block, received=None, after=()):
    count = ids.shape[0]
    rights = [r[None] if r.ndim == 2 else r for r in rights]
    part, column, pieces = piece
    width = rights[0].shape[2] // pieces
    halves = count // 2

    def body(ids_ref, *refs):
        left_refs, right_refs = refs[: len(lefts)], refs[len(lefts) : len(lefts) + len(rights)]
        rest = refs[len(lefts) + len(rights) :]
        left = jnp.concatenate([l[...] for l in left_refs], axis=0) if len(lefts) > 1 else left_refs[0][...]
        total, at = None, 0
        for r in right_refs:
            term = dot(left[at : at + r.shape[1]], r[0], TN)
            at += r.shape[1]
            total = term if total is None else total + term
        if received is None:
            rest[0][0] = total.astype(BF16)
            return
        total = (total + rest[0][0].astype(F32)).astype(BF16)
        i = pl.program_id(0)

        @pl.when(i < halves)
        def _():
            rest[1][0] = total

        @pl.when(i >= halves)
        def _():
            rest[2][0] = total

    ins = [(l, (l.shape[0], block), lambda i, ids: (0, ids[i])) for l in lefts]
    ins += [(r, (1, r.shape[1], width), lambda i, ids: (part, 0, column)) for r in rights]
    shape = (1, block, width)
    if received is None:
        outs = [((count, block, width), BF16, shape, lambda i, ids: (i, 0, 0))]
    else:
        ins.append((received, shape, lambda i, ids: (i, 0, 0)))
        outs = [
            ((halves, block, width), BF16, shape, lambda i, ids: (jnp.minimum(i, halves - 1), 0, 0)),
            ((halves, block, width), BF16, shape, lambda i, ids: (jnp.maximum(i - halves, 0), 0, 0)),
        ]
    rows = sum(l.shape[0] for l in lefts)
    result = call(body, (count,), ins, outs, flops=2 * rows * count * block * width, after=after, prefetch=ids)
    return result[0] if received is None else result


def add_halves(kept, received, after=()):
    count, block, width = kept.shape
    shape = (1, block, width)
    halves = count // 2

    def body(k_ref, r_ref, a_ref, b_ref):
        total = (k_ref[...].astype(F32) + r_ref[...].astype(F32)).astype(BF16)
        i = pl.program_id(0)

        @pl.when(i < halves)
        def _():
            a_ref[...] = total

        @pl.when(i >= halves)
        def _():
            b_ref[...] = total

    return call(
        body,
        (count,),
        [(x, shape, lambda i: (i, 0, 0)) for x in (kept, received)],
        [
            ((halves, block, width), BF16, shape, lambda i: (jnp.minimum(i, halves - 1), 0, 0)),
            ((halves, block, width), BF16, shape, lambda i: (jnp.maximum(i - halves, 0), 0, 0)),
        ],
        flops=kept.size,
        after=after,
    )


def add_last(terms, turn, parts=False, after=()):
    _, block, width = terms[0][0].shape
    count = len(terms)

    def body(*refs):
        for n in range(count):
            total = refs[2 * n][0].astype(F32) + refs[2 * n + 1][0].astype(F32)
            if parts:
                refs[-1][n] = total
            elif turn:
                refs[-1][n * width : (n + 1) * width] = total.T
            else:
                refs[-1][:, n * width : (n + 1) * width] = total

    shape = (count, block, width) if parts else (count * width, block) if turn else (block, count * width)
    return call(
        body,
        (1,),
        [(x, (1, block, width), lambda i: (0, 0, 0)) for pair in terms for x in pair],
        [(shape, F32, shape, lambda i: (0,) * len(shape))],
        flops=2 * block * width,
        after=after,
    )[0]


def unit_of(values):
    centre = values - jnp.mean(values, axis=-1, keepdims=True)
    scaling = lax.rsqrt(jnp.mean(centre * centre, axis=-1, keepdims=True) + 1e-05)
    return centre * scaling, scaling


def rowwise(body, rows_in, whole_in, outs, sums=0, tile=128, after=()):
    rows, depth = rows_in[0].shape
    return call(
        body,
        (rows // tile,),
        [(x, (tile, depth), lambda i: (i, 0)) for x in rows_in]
        + [(x, (1, depth), lambda i: (0, 0)) for x in whole_in],
        [((rows, depth), kind, (tile, depth), lambda i: (i, 0)) for kind in outs]
        + [((1, depth), F32, (1, depth), lambda i: (0, 0))] * sums,
        flops=20 * rows * depth,
        after=after,
    )


def norm_forward(values, gain, shift, after=()):
    def body(v_ref, g_ref, s_ref, o_ref):
        unit, _ = unit_of(v_ref[...].astype(F32))
        o_ref[...] = (unit * g_ref[...] + s_ref[...]).astype(BF16)

    return rowwise(body, [values], [gain, shift], [BF16], after=after)[0]


def sum_norm(base, terms, gain, shift, after=()):
    def body(b_ref, x_ref, y_ref, z_ref, g_ref, s_ref, h_ref, o_ref):
        total = x_ref[...].astype(F32) + y_ref[...].astype(F32) + z_ref[...].astype(F32)
        total = b_ref[...].astype(F32) + total
        h_ref[...] = total
        unit, _ = unit_of(total)
        o_ref[...] = (unit * g_ref[...] + s_ref[...]).astype(BF16)

    return rowwise(body, [base, *terms], [gain, shift], [F32, BF16], after=after)


def sum_low(base, terms, after=()):
    def body(b_ref, x_ref, y_ref, z_ref, o_ref):
        total = x_ref[...].astype(F32) + y_ref[...].astype(F32) + z_ref[...].astype(F32)
        o_ref[...] = (b_ref[...].astype(F32) + total).astype(BF16)

    return rowwise(body, [base, *terms], [], [BF16], after=after)[0]


def norm_back(base, values, terms, gain, keep, after=()):
    def body(b_ref, v_ref, x_ref, y_ref, z_ref, g_ref, o_ref, *rest):
        @pl.when(pl.program_id(0) == 0)
        def _():
            rest[-2][...] = jnp.zeros_like(rest[-2])
            rest[-1][...] = jnp.zeros_like(rest[-1])

        upstream = x_ref[...].astype(F32) + y_ref[...].astype(F32) + z_ref[...].astype(F32)
        unit, scaling = unit_of(v_ref[...].astype(F32))
        rest[-2][...] += jnp.sum(upstream * unit, axis=0, keepdims=True)
        rest[-1][...] += jnp.sum(upstream, axis=0, keepdims=True)
        scaled = upstream * g_ref[...]
        inner = (
            scaled
            - jnp.mean(scaled, axis=-1, keepdims=True)
            - unit * jnp.mean(scaled * unit, axis=-1, keepdims=True)
        )
        total = b_ref[...].astype(F32) + scaling * inner
        o_ref[...] = total.astype(BF16)
        if keep:
            rest[0][...] = total

    return rowwise(
        body, [base, values, *terms], [gain], [BF16, F32] if keep else [BF16], sums=2, after=after
    )


def place(index, pair, rows, so_far=None, after=()):
    block, depth = pair[0].shape
    tile = rows // 4

    def body(i_ref, x_ref, y_ref, *rest):
        where = lax.broadcasted_iota(jnp.int32, (tile, block), 0) + pl.program_id(0) * tile
        total = dot((where == i_ref[:, :block]).astype(BF16), x_ref[...])
        total += dot((where == i_ref[:, block:]).astype(BF16), y_ref[...])
        if so_far is not None:
            total += rest[0][...].astype(F32)
        rest[-1][...] = total.astype(BF16)

    more = [] if so_far is None else [(so_far, (tile, depth), lambda i: (i, 0))]
    return call(
        body,
        (rows // tile,),
        [
            (index, (1, 2 * block), lambda i: (0, 0)),
            (pair[0], (block, depth), lambda i: (0, 0)),
            (pair[1], (block, depth), lambda i: (0, 0)),
            *more,
        ],
        [((rows, depth), BF16, (tile, depth), lambda i: (i, 0))],
        flops=4 * rows * block * depth,
        after=after,
    )[0]


def local(
    n_seq,
    n_head,
    tokens,
    codebook,
    codes,
    modality,
    segments,
    sequence_source,
    w_qkv,
    w_out,
    w_up,
    w_down,
    norm1_gain,
    norm1_shift,
    norm2_gain,
    norm2_shift,
    cotangent,
):
    rows, depth = tokens.shape
    me, own = lax.axis_index("seq"), lax.axis_index("head")
    share = rows // n_seq // n_head
    quarter = rows // n_head
    w3 = jnp.transpose(w_qkv, (1, 0, 2))
    gain1, shift1, gain2, shift2 = [v[None] for v in (norm1_gain, norm1_shift, norm2_gain, norm2_shift)]

    def swap(x, flip, axis="head"):
        size = n_head if axis == "head" else n_seq
        return lax.ppermute(x, axis, [(i, i ^ flip) for i in range(size)])

    def exchange(x):
        return lax.all_to_all(x, "seq", split_axis=0, concat_axis=0, tiled=True)

    source = sequence_source.reshape(n_seq, rows)
    places = jnp.arange(rows, dtype=jnp.int32)
    groups = source // rows
    offsets = source % rows
    leaving = groups == me
    coming = lax.dynamic_index_in_dim(groups, me, 0) == jnp.arange(n_seq, dtype=jnp.int32)[:, None]
    upper = (places[:, None] <= places[None, :]).astype(BF16)
    counts = jnp.dot(
        jnp.concatenate([leaving, coming], axis=0).astype(BF16), upper, preferred_element_type=F32
    ).astype(jnp.int32)
    leaving_rank = jnp.where(leaving, counts[:n_seq] - 1, -1)
    coming_rank = jnp.where(coming, counts[n_seq:] - 1, -1)
    lanes = jnp.arange(share, dtype=jnp.int32)

    def listed(rank, value, blocks):
        wanted = (own ^ jnp.asarray(blocks, jnp.int32))[:, None] * share + lanes[None, :]
        hit = rank[None, :, None, :] == wanted[:, None, :, None]
        return jnp.sum(jnp.where(hit, value[None, :, None, :], 0), axis=-1).reshape(-1)

    sent = listed(leaving_rank, offsets, [0])
    pick = (sent[:, None] == places[None, :]).astype(BF16)
    code = jnp.where(modality == 1, codes, -1)
    sent_code = jnp.sum(jnp.where(sent[:, None] == places[None, :], code[None, :], 0), axis=-1)
    pick_code = (
        sent_code[:, None] == jnp.arange(codebook.shape[0], dtype=jnp.int32)[None, :]
    ).astype(BF16)
    leaving_embedded = (
        jnp.dot(pick, tokens, preferred_element_type=F32)
        + jnp.dot(pick_code, codebook, preferred_element_type=F32)
    ).astype(BF16)
    embedded = exchange(leaving_embedded)

    sent_across = listed(leaving_rank, offsets, [2])
    pick_across = (sent_across[:, None] == places[None, :]).astype(BF16)
    leaving_cot = jnp.concatenate(
        [
            jnp.dot(p, cotangent, preferred_element_type=F32).astype(BF16).reshape(n_seq, share, depth)
            for p in (pick, pick_across)
        ],
        axis=1,
    )
    came = exchange(leaving_cot)
    cot0, cot2 = [came[:, i * share : (i + 1) * share].reshape(quarter, depth) for i in range(2)]
    cot1, cot3 = swap(cot0, 1), swap(cot2, 1)

    sent_all = listed(leaving_rank, offsets, list(range(n_head)))
    segment_row = segments[0]
    begin = jnp.sum((segment_row[:, None] < segment_row[None, :]).astype(jnp.int32), axis=0)
    packed = listed(
        coming_rank, jnp.broadcast_to(begin * rows + places, (n_seq, rows)), list(range(n_head))
    )
    position, start = packed % rows, packed // rows
    pos_col, start_col, pos_row, start_row = position[:, None], start[:, None], position[None], start[None]

    n0 = norm_forward(embedded, gain1, shift1)
    n2 = swap(n0, 2)
    n1 = swap(n0, 1)
    qkv_low = project((n0, n1), w3)
    n2 = gate(n2, qkv_low)
    n3 = swap(n2, 1)
    qkv = (qkv_low, project((n2, n3), w3))
    mixed_out = attend((1, 3), qkv, pos_col, start_col, pos_row)
    a1, a3 = block_matmul(((mixed_out, 0, 2), (mixed_out, 1, 2)), w_out)
    mixed_in = attend((0, 2), qkv, pos_col, start_col, pos_row, after=(a1,))
    a0, passed = block_matmul(((mixed_in, 0, 2), (mixed_in, 1, 2)), w_out, received=swap(a3, 1))
    hidden_in, m0 = sum_norm(embedded, (a0, swap(a1, 1), swap(passed, 2)), gain2, shift2)

    m2 = swap(m0, 2)
    m1 = swap(m0, 1)
    act_low, bar_low = mlp((m0, m1), (cot0, cot1), w_up, w_down)
    m2 = gate(m2, act_low)
    m3 = swap(m2, 1)
    act_high, bar_high = mlp((m2, m3), (cot2, cot3), w_up, w_down)
    bars_out, bars_in = ((bar_low, 1, 2), (bar_high, 1, 2)), ((bar_low, 0, 2), (bar_high, 0, 2))
    acts_out, acts_in = ((act_low, 1, 2), (act_high, 1, 2)), ((act_low, 0, 2), (act_high, 0, 2))

    bits = n_seq.bit_length() - 1
    block = depth // n_seq

    def keep_order(order):
        kept = [0]
        for bit in reversed(order[1:]):
            kept = [k | 1 << bit for k in kept] + kept
        return jnp.asarray(kept, jnp.int32)

    def columns(blocks, ids):
        if block % 128 == 0:
            return blocks, ids, block
        picked = [jnp.take(b.reshape(-1, n_seq, block), ids, axis=1).reshape(b.shape[0], -1) for b in blocks]
        return picked, jnp.arange(n_seq // 2 * block // 128, dtype=jnp.int32), 128

    def first_term(grad, after=()):
        order, lefts, rights, piece = grad
        ids = me ^ (1 << order[0]) ^ keep_order(order)
        blocks, ids, size = columns(lefts, ids)
        made = weight_grad(ids, blocks, rights, piece, size, after=after)
        return swap(made, 1 << order[0], "seq"), made

    def second_term(grad, received, after=()):
        order, lefts, rights, piece = grad
        blocks, ids, size = columns(lefts, me ^ keep_order(order))
        send, keep = weight_grad(ids, blocks, rights, piece, size, received, after=after)
        send, keep = [x.reshape(n_seq // 4, block, x.shape[2]) for x in (send, keep)]
        return swap(send, 1 << order[1], "seq"), keep

    def next_terms(grad, received, keep, after=()):
        for bit in grad[0][2:]:
            send, keep = add_halves(keep, received, after=after)
            received = swap(send, 1 << bit, "seq")
        return received, keep

    straight = list(range(bits))
    turned = [1, 0] + straight[2:]
    cots = (cot0, cot1, cot2, cot3)
    normed_one, normed_two = (n0, n1, n2, n3), (m0, m1, m2, m3)

    acts, bars = (act_low, act_high), (bar_low, bar_high)
    down, up = (straight, cots, acts, (0, 0, 1)), (turned, normed_two, bars, (0, 0, 1))

    down_got, made = first_term(down)
    up_got, made = first_term(up, after=(made,))
    t1, t3 = block_matmul(bars_out, w_up, transposed=True, after=(made,))
    b1, b3 = block_matmul(acts_out, w_down, after=(t1,))
    t0, passed = block_matmul(bars_in, w_up, transposed=True, received=swap(t3, 1), after=(b1,))
    h0, hidden_bar, gain_two, shift_two = norm_back(
        cot0, hidden_in, (t0, swap(t1, 1), swap(passed, 2)), gain2, True
    )
    h2 = swap(h0, 2)
    h1 = swap(h0, 1)

    g0, g1 = block_matmul(((h0, 0, 1), (h1, 0, 1)), w_out, transposed=True)
    b0, branch_passed = block_matmul(acts_in, w_down, received=swap(b3, 1), after=(g0,))
    h2 = gate(h2, branch_passed)
    h3 = swap(h2, 1)
    down_got, down_keep = second_term(down, down_got, after=(h2,))
    g2, g3 = block_matmul(((h2, 0, 1), (h3, 0, 1)), w_out, transposed=True, after=(down_keep, up_got))
    out = (straight, (h1, h3, h0, h2), (mixed_out, mixed_in), (0, 0, 1))
    out_got, made = first_term(out, after=(g2,))
    up_got, up_keep = second_term(up, up_got, after=(made,))
    output_slice = sum_low(hidden_in, (b0, swap(b1, 1), swap(branch_passed, 2)), after=(up_keep,))
    output_home = exchange(output_slice)
    qkv_bar = attend_back(qkv, (g0, g1, g2, g3), pos_col, pos_row, start_row, after=(output_slice,))
    q_grad, k_grad, v_grad = [(straight, normed_one, (qkv_bar,), (n, 0, 1)) for n in range(3)]
    u1, u3 = project_back(qkv_bar, w3, (1, 3), after=(out_got, down_got))
    q_got, made = first_term(q_grad, after=(u1, output_home))
    u0, passed = project_back(qkv_bar, w3, (0, 2), received=swap(u3, 1), after=(made,))
    k_got, made = first_term(k_grad, after=(passed, up_got))
    v_got, made = first_term(v_grad, after=(made,))
    out_got, out_keep = second_term(out, out_got, after=(made,))
    down_got, down_keep = next_terms(down, down_got, down_keep, after=(out_keep,))
    input_slice, gain_one, shift_one = norm_back(
        hidden_bar, embedded, (u0, swap(u1, 1), swap(passed, 2)), gain1, False, after=(down_keep, q_got)
    )
    input_home = exchange(input_slice)
    vectors = jnp.concatenate([gain_one, shift_one, gain_two, shift_two], axis=0)
    vectors = vectors + swap(vectors, 1)
    vectors = vectors + swap(vectors, 2)
    vectors = jnp.transpose(vectors.reshape(4, n_seq, block), (1, 0, 2))
    vectors = jnp.sum(exchange(vectors), axis=0)

    where = [sent_all[None, : 2 * quarter], sent_all[None, 2 * quarter :]]
    x0, x1, x2 = output_home, swap(output_home, 1), swap(output_home, 2)
    up_got, up_keep = next_terms(up, up_got, up_keep, after=(input_slice,))
    q_got, q_keep = second_term(q_grad, q_got, after=(up_keep,))
    first = place(where[0], (x0, x1), rows, after=(q_keep, down_got))
    out_got, out_keep = next_terms(out, out_got, out_keep, after=(first,))
    k_got, k_keep = second_term(k_grad, k_got, after=(out_keep,))
    q_got, q_keep = next_terms(q_grad, q_got, q_keep, after=(k_keep, v_got))
    x2 = gate(x2, q_keep)
    down_grad = add_last([(down_got, down_keep)], True, after=(x2,))
    block_output = place(where[1], (x2, swap(x2, 1)), rows, first, after=(down_grad,))
    y0, y1, y2 = input_home, swap(input_home, 1), swap(input_home, 2)
    v_got, v_keep = second_term(v_grad, v_got, after=(block_output, up_got))
    first = place(where[0], (y0, y1), rows, after=(v_keep,))
    k_got, k_keep = next_terms(k_grad, k_got, k_keep, after=(first,))
    y2 = gate(y2, k_keep, out_got, q_got)
    up_grad = add_last([(up_got, up_keep)], False, after=(y2,))
    input_grad = place(where[1], (y2, swap(y2, 1)), rows, first, after=(up_grad,))
    v_got, v_keep = next_terms(v_grad, v_got, v_keep, after=(input_grad,))
    out_grad = add_last([(out_got, out_keep)], True, after=(v_keep,))
    qkv_grad = add_last(
        [(q_got, q_keep), (k_got, k_keep), (v_got, v_keep)], False, True, after=(out_grad,)
    )
    qkv_grad = jnp.transpose(qkv_grad, (1, 0, 2))

    return (
        block_output,
        input_grad,
        qkv_grad,
        out_grad,
        up_grad,
        down_grad,
        vectors[0],
        vectors[1],
        vectors[2],
        vectors[3],
    )


def solution(mesh):
    return jax.shard_map(
        partial(local, mesh.shape["seq"], mesh.shape["head"]),
        mesh=mesh,
        in_specs=(
            P("seq", None),
            P(),
            P("seq"),
            P("seq"),
            P("seq", None),
            P(),
            P(None, None, "head"),
            P("head", None),
            P(None, "head"),
            P("head", None),
            P(),
            P(),
            P(),
            P(),
            P("seq", None),
        ),
        out_specs=(
            P("seq", None),
            P("seq", None),
            P("seq", None, "head"),
            P("head", "seq"),
            P("seq", "head"),
            P("head", "seq"),
            P("seq"),
            P("seq"),
            P("seq"),
            P("seq"),
        ),
        check_vma=False,
    )
```

```python
from functools import partial
import math

import jax
import jax.numpy as jnp
from jax import lax
from jax.experimental import pallas as pl
from jax.experimental.pallas import tpu as pltpu
from jax.sharding import PartitionSpec as P

HEAD_DIM = 128
F32 = jnp.float32
BF16 = jnp.bfloat16
MIB = 1 << 20
NN = ((1,), (0,))
NT = ((1,), (1,))
TN = ((0,), (0,))


def dot(a, b, contract=NN):
    return lax.dot_general(a, b, (contract, ((), ())), preferred_element_type=F32)


def call(body, grid, ins, outs, scratch=(), flops=0, special=0, after=(), prefetch=None):
    arrays = [array for array, _, _ in ins]
    specs = [pl.BlockSpec(block, index) for _, block, index in ins] + [pl.BlockSpec(memory_space=pl.ANY)] * len(after)
    shapes = [jax.ShapeDtypeStruct(shape, kind) for shape, kind, _, _ in outs]
    n_in, n_pre = len(ins), 0 if prefetch is None else 1

    def wrapped(*refs):
        body(*refs[: n_pre + n_in], *refs[n_pre + n_in + len(after) :])

    moved = sum(a.size * a.dtype.itemsize for a in arrays) + sum(s.size * s.dtype.itemsize for s in shapes)
    out_specs = [pl.BlockSpec(block, index) for _, _, block, index in outs]
    keys = dict(
        out_shape=shapes,
        compiler_params=pltpu.CompilerParams(vmem_limit_bytes=55 * MIB),
        cost_estimate=pl.CostEstimate(flops=0, bytes_accessed=0, transcendentals=0),
    )
    if prefetch is None:
        made = pl.pallas_call(
            wrapped, grid=grid, in_specs=specs, out_specs=out_specs, scratch_shapes=list(scratch), **keys
        )
        return made(*arrays, *after)
    spec = pltpu.PrefetchScalarGridSpec(
        num_scalar_prefetch=1, grid=grid, in_specs=specs, out_specs=out_specs, scratch_shapes=list(scratch)
    )
    return pl.pallas_call(wrapped, grid_spec=spec, **keys)(prefetch, *arrays, *after)


def gate(x, *after):
    def body(*refs):
        pass

    anywhere = pl.BlockSpec(memory_space=pl.ANY)
    return pl.pallas_call(
        body,
        in_specs=[anywhere] * (1 + len(after)),
        out_specs=anywhere,
        out_shape=jax.ShapeDtypeStruct(x.shape, x.dtype),
        input_output_aliases={0: 0},
        cost_estimate=pl.CostEstimate(flops=0, bytes_accessed=0, transcendentals=0),
    )(x, *after)


def block_matmul(picks, b, transposed=False, tile=512, received=None, after=()):
    rows, depth = picks[0][0].shape[0] // picks[0][2], picks[0][0].shape[1]
    width = b.shape[0] if transposed else b.shape[1]

    def body(x_ref, y_ref, b_ref, *rest):
        o_ref, p_ref, both = rest[-3:]

        @pl.when(pl.program_id(0) == 0)
        def _():
            both[:rows] = x_ref[...]
            both[rows:] = y_ref[...]

        result = dot(both[...], b_ref[...], NT if transposed else NN)
        o_ref[...] = result[:rows].astype(BF16)
        second = result[rows:]
        if received is not None:
            second += rest[0][...].astype(F32)
        p_ref[...] = second.astype(BF16)

    side = ((tile, depth), lambda j: (j, 0)) if transposed else ((depth, tile), lambda j: (0, j))
    more = [] if received is None else [(received, (rows, tile), lambda j: (0, j))]
    return call(
        body,
        (width // tile,),
        [(x, (rows, depth), lambda j, n=n: (n, 0)) for x, n, _ in picks] + [(b, *side)] + more,
        [((rows, width), BF16, (rows, tile), lambda j: (0, j))] * 2,
        [pltpu.VMEM((2 * rows, depth), BF16)],
        flops=4 * rows * width * depth,
        after=after,
    )


def project(pair, w3, after=()):
    rows, depth = pair[0].shape
    width = w3.shape[2]

    def body(x_ref, y_ref, w_ref, o_ref, both):
        @pl.when(pl.program_id(0) == 0)
        def _():
            both[:rows] = x_ref[...]
            both[rows:] = y_ref[...]

        o_ref[0] = dot(both[...], w_ref[0]).astype(BF16)

    return call(
        body,
        (3,),
        [(x, (rows, depth), lambda s: (0, 0)) for x in pair]
        + [(w3, (1, depth, width), lambda s: (s, 0, 0))],
        [((3, 2 * rows, width), BF16, (1, 2 * rows, width), lambda s: (s, 0, 0))],
        [pltpu.VMEM((2 * rows, depth), BF16)],
        flops=12 * rows * width * depth,
        after=after,
    )[0]


def project_back(g3, w3, picks, tile=512, received=None, after=()):
    width, depth, rows = g3.shape[2], w3.shape[1], g3.shape[1] // 4

    def body(x_ref, y_ref, w_ref, *rest):
        o_ref, p_ref, both = rest[-3:]

        @pl.when(pl.program_id(0) == 0)
        def _():
            both[:, :rows] = x_ref[...]
            both[:, rows:] = y_ref[...]

        total = dot(both[0], w_ref[0], NT)
        total += dot(both[1], w_ref[1], NT)
        total += dot(both[2], w_ref[2], NT)
        o_ref[...] = total[:rows].astype(BF16)
        second = total[rows:]
        if received is not None:
            second += rest[0][...].astype(F32)
        p_ref[...] = second.astype(BF16)

    more = [] if received is None else [(received, (rows, tile), lambda j: (0, j))]
    return call(
        body,
        (depth // tile,),
        [(g3, (3, rows, width), lambda j, n=n: (0, n, 0)) for n in picks]
        + [(w3, (3, tile, width), lambda j: (0, j, 0))]
        + more,
        [((rows, depth), BF16, (rows, tile), lambda j: (0, j))] * 2,
        [pltpu.VMEM((3, 2 * rows, width), BF16)],
        flops=12 * rows * width * depth,
        after=after,
    )


def mlp(normed, cot, w_up, w_down, tile=512, after=()):
    rows, depth = normed[0].shape
    width = w_up.shape[1]

    def body(n0, n1, c0, c1, u_ref, d_ref, act_ref, bar_ref, n_both, c_both):
        @pl.when(pl.program_id(0) == 0)
        def _():
            n_both[:rows] = n0[...]
            n_both[rows:] = n1[...]
            c_both[:rows] = c0[...]
            c_both[rows:] = c1[...]

        up = dot(n_both[...], u_ref[...])
        grad = dot(c_both[...], d_ref[...], NT)
        bell = jnp.exp(up * up * -0.5)
        t = 1.0 / (1.0 + (0.3275911 / math.sqrt(2.0)) * jnp.abs(up))
        poly = t * (
            0.127414796 + t * (-0.142248368 + t * (0.7107068705 + t * (-0.7265760135 + t * 0.5307027145)))
        )
        tail = poly * bell
        phi = jnp.where(up < 0.0, tail, 1.0 - tail)
        act_ref[...] = (up * phi).astype(BF16)
        slope = phi + up * bell * (1.0 / math.sqrt(2.0 * math.pi))
        bar_ref[...] = (slope * grad).astype(BF16)

    return call(
        body,
        (width // tile,),
        [(x, (rows, depth), lambda j: (0, 0)) for x in (*normed, *cot)]
        + [(w_up, (depth, tile), lambda j: (0, j)), (w_down, (tile, depth), lambda j: (j, 0))],
        [((2 * rows, width), BF16, (2 * rows, tile), lambda j: (0, j))] * 2,
        [pltpu.VMEM((2 * rows, depth), BF16)] * 2,
        flops=8 * rows * width * depth,
        special=4 * rows * width,
        after=after,
    )


def attend(picks, qkv, pos_col, start_col, pos_row, after=()):
    _, half, width = qkv[0].shape
    rows = half // 2
    heads = width // HEAD_DIM
    factor = 1.0 / math.sqrt(HEAD_DIM)

    def body(x_ref, y_ref, low_ref, high_ref, px_ref, py_ref, sx_ref, sy_ref, pr_ref, o_ref, kv, both):
        i = pl.program_id(0)

        @pl.when(i == 0)
        def _():
            kv[:, :half] = low_ref[1:]
            kv[:, half:] = high_ref[1:]
            both[0] = x_ref[0]
            both[1] = y_ref[0]

        keys = pr_ref[...]
        at = jnp.where(i == 0, px_ref[...], py_ref[...])
        since = jnp.where(i == 0, sx_ref[...], sy_ref[...])
        bias = jnp.where((keys <= at) & (keys >= since), 0.0, -1e30)
        for head in range(heads):
            cols = slice(head * HEAD_DIM, (head + 1) * HEAD_DIM)
            scores = dot(both[i, :, cols], kv[0, :, cols], NT) * factor + bias
            peak = jnp.max(scores, axis=-1, keepdims=True)
            grown = jnp.exp(scores - peak)
            total = jnp.sum(grown, axis=-1, keepdims=True)
            o_ref[:, cols] = (dot(grown.astype(BF16), kv[1, :, cols]) * (1.0 / total)).astype(BF16)

    return call(
        body,
        (2,),
        [(qkv[n // 2], (1, rows, width), lambda i, n=n: (0, n % 2, 0)) for n in picks]
        + [
            (qkv[0], (3, half, width), lambda i: (0, 0, 0)),
            (qkv[1], (3, half, width), lambda i: (0, 0, 0)),
        ]
        + [(c, (rows, 1), lambda i, n=n: (n, 0)) for c in (pos_col, start_col) for n in picks]
        + [(pos_row, (1, 2 * half), lambda i: (0, 0))],
        [((half, width), BF16, (rows, width), lambda i: (i, 0))],
        [pltpu.VMEM((2, 2 * half, width), BF16), pltpu.VMEM((2, rows, width), BF16)],
        flops=8 * half * half * width,
        special=2 * heads * half * half,
        after=after,
    )[0]


def attend_back(qkv, bars, pos_col, pos_row, start_row, after=()):
    _, half, width = qkv[0].shape
    rows = 2 * half
    tile = rows // 4
    heads = width // HEAD_DIM
    factor = 1.0 / math.sqrt(HEAD_DIM)

    def body(low_ref, high_ref, g0, g1, g2, g3, pc_ref, pr_ref, sr_ref, o_ref, all_qkv, dk, dv, g_tile):
        step = pl.program_id(0)
        keys = pc_ref[...]
        seen = (keys <= pr_ref[...]) & (keys >= sr_ref[...])
        bias = jnp.where(seen, 0.0, -1e30)

        @pl.when(step == 0)
        def _():
            dk[...] = jnp.zeros_like(dk)
            dv[...] = jnp.zeros_like(dv)
            all_qkv[:, :half] = low_ref[...]
            all_qkv[:, half:] = high_ref[...]

        for number, g_ref in enumerate((g0, g1, g2, g3)):

            @pl.when(step == number)
            def _():
                g_tile[...] = g_ref[...]

        here = pl.ds(pl.multiple_of(step * tile, tile), tile)
        for head in range(heads):
            cols = slice(head * HEAD_DIM, (head + 1) * HEAD_DIM)
            q, k, v, g = all_qkv[0, here, cols], all_qkv[1, :, cols], all_qkv[2, :, cols], g_tile[:, cols]
            scores = dot(k, q, NT) * factor + bias
            peak = jnp.max(scores, axis=0, keepdims=True)
            grown = jnp.exp(scores - peak)
            probs = grown * (1.0 / jnp.sum(grown, axis=0, keepdims=True))
            dv[:, cols] += dot(probs.astype(BF16), g)
            probs_bar = dot(v, g, NT)
            inner = jnp.sum(probs * probs_bar, axis=0, keepdims=True)
            scores_bar = (probs * (probs_bar - inner)).astype(BF16)
            dk[:, cols] += dot(scores_bar, q)
            dq = dot(scores_bar, k, TN) * factor
            o_ref[0, here, cols] = dq.astype(BF16)

        @pl.when(step == pl.num_programs(0) - 1)
        def _():
            o_ref[1] = (dk[...] * factor).astype(BF16)
            o_ref[2] = dv[...].astype(BF16)

    return call(
        body,
        (4,),
        [
            (qkv[0], (3, half, width), lambda i: (0, 0, 0)),
            (qkv[1], (3, half, width), lambda i: (0, 0, 0)),
            *[(bar, (tile, width), lambda i: (0, 0)) for bar in bars],
            (pos_col, (rows, 1), lambda i: (0, 0)),
            (pos_row, (1, tile), lambda i: (0, i)),
            (start_row, (1, tile), lambda i: (0, i)),
        ],
        [((3, rows, width), BF16, (3, rows, width), lambda i: (0, 0, 0))],
        [
            pltpu.VMEM((3, rows, width), BF16),
            pltpu.VMEM((rows, width), F32),
            pltpu.VMEM((rows, width), F32),
            pltpu.VMEM((tile, width), BF16),
        ],
        flops=10 * rows * rows * width,
        special=heads * rows * rows,
        after=after,
    )[0]


def weight_grad(ids, lefts, rights, piece, block, received=None, after=()):
    count = ids.shape[0]
    rights = [r[None] if r.ndim == 2 else r for r in rights]
    part, column, pieces = piece
    width = rights[0].shape[2] // pieces
    halves = count // 2

    def body(ids_ref, *refs):
        left_refs, right_refs = refs[: len(lefts)], refs[len(lefts) : len(lefts) + len(rights)]
        rest = refs[len(lefts) + len(rights) :]
        left = jnp.concatenate([l[...] for l in left_refs], axis=0) if len(lefts) > 1 else left_refs[0][...]
        total, at = None, 0
        for r in right_refs:
            term = dot(left[at : at + r.shape[1]], r[0], TN)
            at += r.shape[1]
            total = term if total is None else total + term
        if received is None:
            rest[0][0] = total.astype(BF16)
            return
        total = (total + rest[0][0].astype(F32)).astype(BF16)
        i = pl.program_id(0)

        @pl.when(i < halves)
        def _():
            rest[1][0] = total

        @pl.when(i >= halves)
        def _():
            rest[2][0] = total

    ins = [(l, (l.shape[0], block), lambda i, ids: (0, ids[i])) for l in lefts]
    ins += [(r, (1, r.shape[1], width), lambda i, ids: (part, 0, column)) for r in rights]
    shape = (1, block, width)
    if received is None:
        outs = [((count, block, width), BF16, shape, lambda i, ids: (i, 0, 0))]
    else:
        ins.append((received, shape, lambda i, ids: (i, 0, 0)))
        outs = [
            ((halves, block, width), BF16, shape, lambda i, ids: (jnp.minimum(i, halves - 1), 0, 0)),
            ((halves, block, width), BF16, shape, lambda i, ids: (jnp.maximum(i - halves, 0), 0, 0)),
        ]
    rows = sum(l.shape[0] for l in lefts)
    result = call(body, (count,), ins, outs, flops=2 * rows * count * block * width, after=after, prefetch=ids)
    return result[0] if received is None else result


def add_halves(kept, received, after=()):
    count, block, width = kept.shape
    shape = (1, block, width)
    halves = count // 2

    def body(k_ref, r_ref, a_ref, b_ref):
        total = (k_ref[...].astype(F32) + r_ref[...].astype(F32)).astype(BF16)
        i = pl.program_id(0)

        @pl.when(i < halves)
        def _():
            a_ref[...] = total

        @pl.when(i >= halves)
        def _():
            b_ref[...] = total

    return call(
        body,
        (count,),
        [(x, shape, lambda i: (i, 0, 0)) for x in (kept, received)],
        [
            ((halves, block, width), BF16, shape, lambda i: (jnp.minimum(i, halves - 1), 0, 0)),
            ((halves, block, width), BF16, shape, lambda i: (jnp.maximum(i - halves, 0), 0, 0)),
        ],
        flops=kept.size,
        after=after,
    )


def add_last(terms, turn, parts=False, after=()):
    _, block, width = terms[0][0].shape
    count = len(terms)

    def body(*refs):
        for n in range(count):
            total = refs[2 * n][0].astype(F32) + refs[2 * n + 1][0].astype(F32)
            if parts:
                refs[-1][n] = total
            elif turn:
                refs[-1][n * width : (n + 1) * width] = total.T
            else:
                refs[-1][:, n * width : (n + 1) * width] = total

    shape = (count, block, width) if parts else (count * width, block) if turn else (block, count * width)
    return call(
        body,
        (1,),
        [(x, (1, block, width), lambda i: (0, 0, 0)) for pair in terms for x in pair],
        [(shape, F32, shape, lambda i: (0,) * len(shape))],
        flops=2 * block * width,
        after=after,
    )[0]


def unit_of(values):
    centre = values - jnp.mean(values, axis=-1, keepdims=True)
    scaling = lax.rsqrt(jnp.mean(centre * centre, axis=-1, keepdims=True) + 1e-05)
    return centre * scaling, scaling


def rowwise(body, rows_in, whole_in, outs, sums=0, tile=128, after=()):
    rows, depth = rows_in[0].shape
    return call(
        body,
        (rows // tile,),
        [(x, (tile, depth), lambda i: (i, 0)) for x in rows_in]
        + [(x, (1, depth), lambda i: (0, 0)) for x in whole_in],
        [((rows, depth), kind, (tile, depth), lambda i: (i, 0)) for kind in outs]
        + [((1, depth), F32, (1, depth), lambda i: (0, 0))] * sums,
        flops=20 * rows * depth,
        after=after,
    )


def norm_forward(values, gain, shift, after=()):
    def body(v_ref, g_ref, s_ref, o_ref):
        unit, _ = unit_of(v_ref[...].astype(F32))
        o_ref[...] = (unit * g_ref[...] + s_ref[...]).astype(BF16)

    return rowwise(body, [values], [gain, shift], [BF16], after=after)[0]


def sum_norm(base, terms, gain, shift, after=()):
    def body(b_ref, x_ref, y_ref, z_ref, g_ref, s_ref, h_ref, o_ref):
        total = x_ref[...].astype(F32) + y_ref[...].astype(F32) + z_ref[...].astype(F32)
        total = b_ref[...].astype(F32) + total
        h_ref[...] = total
        unit, _ = unit_of(total)
        o_ref[...] = (unit * g_ref[...] + s_ref[...]).astype(BF16)

    return rowwise(body, [base, *terms], [gain, shift], [F32, BF16], after=after)


def sum_low(base, terms, after=()):
    def body(b_ref, x_ref, y_ref, z_ref, o_ref):
        total = x_ref[...].astype(F32) + y_ref[...].astype(F32) + z_ref[...].astype(F32)
        o_ref[...] = (b_ref[...].astype(F32) + total).astype(BF16)

    return rowwise(body, [base, *terms], [], [BF16], after=after)[0]


def norm_back(base, values, terms, gain, keep, after=()):
    def body(b_ref, v_ref, x_ref, y_ref, z_ref, g_ref, o_ref, *rest):
        @pl.when(pl.program_id(0) == 0)
        def _():
            rest[-2][...] = jnp.zeros_like(rest[-2])
            rest[-1][...] = jnp.zeros_like(rest[-1])

        upstream = x_ref[...].astype(F32) + y_ref[...].astype(F32) + z_ref[...].astype(F32)
        unit, scaling = unit_of(v_ref[...].astype(F32))
        rest[-2][...] += jnp.sum(upstream * unit, axis=0, keepdims=True)
        rest[-1][...] += jnp.sum(upstream, axis=0, keepdims=True)
        scaled = upstream * g_ref[...]
        inner = (
            scaled
            - jnp.mean(scaled, axis=-1, keepdims=True)
            - unit * jnp.mean(scaled * unit, axis=-1, keepdims=True)
        )
        total = b_ref[...].astype(F32) + scaling * inner
        o_ref[...] = total.astype(BF16)
        if keep:
            rest[0][...] = total

    return rowwise(
        body, [base, values, *terms], [gain], [BF16, F32] if keep else [BF16], sums=2, after=after
    )


def place(index, pair, rows, so_far=None, after=()):
    block, depth = pair[0].shape
    tile = rows // 4

    def body(i_ref, x_ref, y_ref, *rest):
        where = lax.broadcasted_iota(jnp.int32, (tile, block), 0) + pl.program_id(0) * tile
        total = dot((where == i_ref[:, :block]).astype(BF16), x_ref[...])
        total += dot((where == i_ref[:, block:]).astype(BF16), y_ref[...])
        if so_far is not None:
            total += rest[0][...].astype(F32)
        rest[-1][...] = total.astype(BF16)

    more = [] if so_far is None else [(so_far, (tile, depth), lambda i: (i, 0))]
    return call(
        body,
        (rows // tile,),
        [
            (index, (1, 2 * block), lambda i: (0, 0)),
            (pair[0], (block, depth), lambda i: (0, 0)),
            (pair[1], (block, depth), lambda i: (0, 0)),
            *more,
        ],
        [((rows, depth), BF16, (tile, depth), lambda i: (i, 0))],
        flops=4 * rows * block * depth,
        after=after,
    )[0]


PLAN = (
    "fD",
    "fU",
    "KA",
    "KB",
    "BA",
    "NB",
    "GL",
    "BB",
    "GG",
    "sD",
    "GH",
    "fO",
    "sU",
    "OS",
    "AT",
    "aD",
    "KA1 O.y",
    "fQ b2",
    "KB1 x0",
    "fK U.z",
    "fV",
    "NB1 Q.y",
    "sO",
    "aU D.l",
    "sQ",
    "OL v",
    "aO",
    "sK",
    "aQ V.y",
    "sV",
    "aK",
    "GX U.l O.l V.z",
    "DE",
    "OH",
    "IL Q.l",
    "aV K.l",
    "GY w",
    "UE",
    "IH",
    "OE",
    "QE",
)


def local(
    n_seq,
    n_head,
    tokens,
    codebook,
    codes,
    modality,
    segments,
    sequence_source,
    w_qkv,
    w_out,
    w_up,
    w_down,
    norm1_gain,
    norm1_shift,
    norm2_gain,
    norm2_shift,
    cotangent,
):
    rows, depth = tokens.shape
    me, own = lax.axis_index("seq"), lax.axis_index("head")
    share = rows // n_seq // n_head
    quarter = rows // n_head
    w3 = jnp.transpose(w_qkv, (1, 0, 2))
    gain1, shift1, gain2, shift2 = [v[None] for v in (norm1_gain, norm1_shift, norm2_gain, norm2_shift)]

    def swap(x, flip, axis="head"):
        size = n_head if axis == "head" else n_seq
        return lax.ppermute(x, axis, [(i, i ^ flip) for i in range(size)])

    def exchange(x):
        return lax.all_to_all(x, "seq", split_axis=0, concat_axis=0, tiled=True)

    source = sequence_source.reshape(n_seq, rows)
    places = jnp.arange(rows, dtype=jnp.int32)
    groups = source // rows
    offsets = source % rows
    leaving = groups == me
    coming = lax.dynamic_index_in_dim(groups, me, 0) == jnp.arange(n_seq, dtype=jnp.int32)[:, None]
    upper = (places[:, None] <= places[None, :]).astype(BF16)
    counts = jnp.dot(
        jnp.concatenate([leaving, coming], axis=0).astype(BF16), upper, preferred_element_type=F32
    ).astype(jnp.int32)
    leaving_rank = jnp.where(leaving, counts[:n_seq] - 1, -1)
    coming_rank = jnp.where(coming, counts[n_seq:] - 1, -1)
    lanes = jnp.arange(share, dtype=jnp.int32)

    def listed(rank, value, blocks):
        wanted = (own ^ jnp.asarray(blocks, jnp.int32))[:, None] * share + lanes[None, :]
        hit = rank[None, :, None, :] == wanted[:, None, :, None]
        return jnp.sum(jnp.where(hit, value[None, :, None, :], 0), axis=-1).reshape(-1)

    sent = listed(leaving_rank, offsets, [0])
    pick = (sent[:, None] == places[None, :]).astype(BF16)
    code = jnp.where(modality == 1, codes, -1)
    sent_code = jnp.sum(jnp.where(sent[:, None] == places[None, :], code[None, :], 0), axis=-1)
    pick_code = (
        sent_code[:, None] == jnp.arange(codebook.shape[0], dtype=jnp.int32)[None, :]
    ).astype(BF16)
    leaving_embedded = (
        jnp.dot(pick, tokens, preferred_element_type=F32)
        + jnp.dot(pick_code, codebook, preferred_element_type=F32)
    ).astype(BF16)
    embedded = exchange(leaving_embedded)

    sent_across = listed(leaving_rank, offsets, [2])
    pick_across = (sent_across[:, None] == places[None, :]).astype(BF16)
    leaving_cot = jnp.concatenate(
        [
            jnp.dot(p, cotangent, preferred_element_type=F32).astype(BF16).reshape(n_seq, share, depth)
            for p in (pick, pick_across)
        ],
        axis=1,
    )
    came = exchange(leaving_cot)
    cot0, cot2 = [came[:, i * share : (i + 1) * share].reshape(quarter, depth) for i in range(2)]
    cot1, cot3 = swap(cot0, 1), swap(cot2, 1)

    sent_all = listed(leaving_rank, offsets, list(range(n_head)))
    segment_row = segments[0]
    begin = jnp.sum((segment_row[:, None] < segment_row[None, :]).astype(jnp.int32), axis=0)
    packed = listed(
        coming_rank, jnp.broadcast_to(begin * rows + places, (n_seq, rows)), list(range(n_head))
    )
    position, start = packed % rows, packed // rows
    pos_col, start_col, pos_row, start_row = position[:, None], start[:, None], position[None], start[None]

    n0 = norm_forward(embedded, gain1, shift1)
    n2 = swap(n0, 2)
    n1 = swap(n0, 1)
    qkv_low = project((n0, n1), w3)
    n2 = gate(n2, qkv_low)
    n3 = swap(n2, 1)
    qkv = (qkv_low, project((n2, n3), w3))
    mixed_out = attend((1, 3), qkv, pos_col, start_col, pos_row)
    a1, a3 = block_matmul(((mixed_out, 0, 2), (mixed_out, 1, 2)), w_out)
    mixed_in = attend((0, 2), qkv, pos_col, start_col, pos_row, after=(a1,))
    a0, passed = block_matmul(((mixed_in, 0, 2), (mixed_in, 1, 2)), w_out, received=swap(a3, 1))
    hidden_in, m0 = sum_norm(embedded, (a0, swap(a1, 1), swap(passed, 2)), gain2, shift2)

    m2 = swap(m0, 2)
    m1 = swap(m0, 1)
    act_low, bar_low = mlp((m0, m1), (cot0, cot1), w_up, w_down)
    m2 = gate(m2, act_low)
    m3 = swap(m2, 1)
    act_high, bar_high = mlp((m2, m3), (cot2, cot3), w_up, w_down)
    bars_out, bars_in = ((bar_low, 1, 2), (bar_high, 1, 2)), ((bar_low, 0, 2), (bar_high, 0, 2))
    acts_out, acts_in = ((act_low, 1, 2), (act_high, 1, 2)), ((act_low, 0, 2), (act_high, 0, 2))

    bits = n_seq.bit_length() - 1
    block = depth // n_seq

    def keep_order(order):
        kept = [0]
        for bit in reversed(order[1:]):
            kept = [k | 1 << bit for k in kept] + kept
        return jnp.asarray(kept, jnp.int32)

    def columns(blocks, ids):
        if block % 128 == 0:
            return blocks, ids, block
        picked = [jnp.take(b.reshape(-1, n_seq, block), ids, axis=1).reshape(b.shape[0], -1) for b in blocks]
        return picked, jnp.arange(n_seq // 2 * block // 128, dtype=jnp.int32), 128

    def first_term(grad, after=()):
        order, lefts, rights, piece = grad
        ids = me ^ (1 << order[0]) ^ keep_order(order)
        blocks, ids, size = columns(lefts, ids)
        made = weight_grad(ids, blocks, rights, piece, size, after=after)
        return swap(made, 1 << order[0], "seq"), made

    def second_term(grad, received, after=()):
        order, lefts, rights, piece = grad
        blocks, ids, size = columns(lefts, me ^ keep_order(order))
        send, keep = weight_grad(ids, blocks, rights, piece, size, received, after=after)
        send, keep = [x.reshape(n_seq // 4, block, x.shape[2]) for x in (send, keep)]
        return swap(send, 1 << order[1], "seq"), keep

    def next_terms(grad, received, keep, after=()):
        for bit in grad[0][2:]:
            send, keep = add_halves(keep, received, after=after)
            received = swap(send, 1 << bit, "seq")
        return received, keep

    straight = list(range(bits))
    turned = [1, 0] + straight[2:]
    cots = (cot0, cot1, cot2, cot3)
    normed_one, normed_two = (n0, n1, n2, n3), (m0, m1, m2, m3)

    acts, bars = (act_low, act_high), (bar_low, bar_high)
    have = {}
    grads = {
        "D": (straight, cots, acts, (0, 0, 1)),
        "U": (turned, normed_two, bars, (0, 0, 1)),
    }
    where = [sent_all[None, : 2 * quarter], sent_all[None, 2 * quarter :]]

    def first(name, after):
        have[name + ".y"], made = first_term(grads[name], after)
        return made

    def second(name, after):
        have[name + ".z"], have[name + ".k"] = second_term(grads[name], have[name + ".y"], after)
        return have[name + ".k"]

    def add(name, after):
        have[name + ".l"], have[name + ".m"] = next_terms(grads[name], have[name + ".z"], have[name + ".k"], after)
        return have[name + ".m"]

    def last(name):
        return have[name + ".l"], have[name + ".m"]

    def near_up(after):
        t1, t3 = block_matmul(bars_out, w_up, transposed=True, after=after)
        have["t1"], have["t3"] = swap(t1, 1), swap(t3, 1)
        return t1

    def near_branch(after):
        b1, b3 = block_matmul(acts_out, w_down, after=after)
        have["b1"], have["b3"] = swap(b1, 1), swap(b3, 1)
        return b1

    def far_up(after):
        have["t0"], passed = block_matmul(bars_in, w_up, transposed=True, received=have["t3"], after=after)
        have["t2"] = swap(passed, 2)
        return passed

    def far_branch(after):
        have["b0"], passed = block_matmul(acts_in, w_down, received=have["b3"], after=after)
        have["b2"] = swap(passed, 2)
        return passed

    def hidden(after):
        h0, have["hidden_bar"], have["gain_two"], have["shift_two"] = norm_back(
            cot0, hidden_in, (have["t0"], have["t1"], have["t2"]), gain2, True, after=after
        )
        have["h0"], have["h2"], have["h1"] = h0, swap(h0, 2), swap(h0, 1)
        return h0

    def context_low(after):
        have["g0"], have["g1"] = block_matmul(
            ((have["h0"], 0, 1), (have["h1"], 0, 1)), w_out, transposed=True, after=after
        )
        return have["g1"]

    def gate_hidden(after):
        have["h2"] = gate(have["h2"], *after)
        have["h3"] = swap(have["h2"], 1)
        grads["O"] = (
            straight,
            (have["h1"], have["h3"], have["h0"], have["h2"]),
            (mixed_out, mixed_in),
            (0, 0, 1),
        )
        return have["h2"]

    def context_high(after):
        have["g2"], have["g3"] = block_matmul(
            ((have["h2"], 0, 1), (have["h3"], 0, 1)), w_out, transposed=True, after=after
        )
        return have["g3"]

    def output(after):
        made = sum_low(hidden_in, (have["b0"], have["b1"], have["b2"]), after=after)
        home = exchange(made)
        have["x0"], have["x1"], have["x2"] = home, swap(home, 1), swap(home, 2)
        return made

    def attention(after):
        made = attend_back(
            qkv, [have[g] for g in ("g0", "g1", "g2", "g3")], pos_col, pos_row, start_row, after=after
        )
        for n, name in enumerate(("Q", "K", "V")):
            grads[name] = (straight, normed_one, (made,), (n, 0, 1))
        have["qkv_bar"] = made
        return made

    def near_input(after):
        u1, u3 = project_back(have["qkv_bar"], w3, (1, 3), after=after)
        have["u1"], have["u3"] = swap(u1, 1), swap(u3, 1)
        return u1

    def far_input(after):
        have["u0"], passed = project_back(have["qkv_bar"], w3, (0, 2), received=have["u3"], after=after)
        have["u2"] = swap(passed, 2)
        return passed

    def inputs(after):
        made, gain_one, shift_one = norm_back(
            have["hidden_bar"], embedded, (have["u0"], have["u1"], have["u2"]), gain1, False, after=after
        )
        home = exchange(made)
        have["y0"], have["y1"], have["y2"] = home, swap(home, 1), swap(home, 2)
        vectors = jnp.concatenate([gain_one, shift_one, have["gain_two"], have["shift_two"]], axis=0)
        vectors = vectors + swap(vectors, 1)
        have["v"] = vectors + swap(vectors, 2)
        have["w"] = exchange(jnp.transpose(have["v"].reshape(4, n_seq, block), (1, 0, 2)))
        return made

    def place_low(out, x, after):
        have[out] = place(where[0], (have[x + "0"], have[x + "1"]), rows, after=after)
        return have[out]

    def gate_across(x, after):
        have[x + "2"] = gate(have[x + "2"], *after)
        have[x + "3"] = swap(have[x + "2"], 1)
        return have[x + "2"]

    def place_high(out, x, after):
        have[out] = place(where[1], (have[x + "2"], have[x + "3"]), rows, have[out], after=after)
        return have[out]

    def down_end(after):
        have["down"] = add_last([last("D")], True, after=after)
        return have["down"]

    def up_end(after):
        have["up"] = add_last([last("U")], False, after=after)
        return have["up"]

    def out_end(after):
        have["out"] = add_last([last("O")], True, after=after)
        return have["out"]

    def qkv_end(after):
        have["qkv"] = add_last([last("Q"), last("K"), last("V")], False, True, after=after)
        return have["qkv"]

    steps = {
        "KA": near_up,
        "BA": near_branch,
        "KB": far_up,
        "NB": hidden,
        "GL": context_low,
        "BB": far_branch,
        "GG": gate_hidden,
        "GH": context_high,
        "OS": output,
        "AT": attention,
        "KA1": near_input,
        "KB1": far_input,
        "NB1": inputs,
        "OL": partial(place_low, "output", "x"),
        "GX": partial(gate_across, "x"),
        "OH": partial(place_high, "output", "x"),
        "IL": partial(place_low, "input", "y"),
        "GY": partial(gate_across, "y"),
        "IH": partial(place_high, "input", "y"),
        "DE": down_end,
        "UE": up_end,
        "OE": out_end,
        "QE": qkv_end,
    }
    for name in "DUOQKV":
        steps["f" + name] = partial(first, name)
        steps["s" + name] = partial(second, name)
        steps["a" + name] = partial(add, name)
    made = None
    for line in PLAN:
        step, *arrivals = line.split()
        after = () if made is None else (made,)
        made = steps[step](after + tuple(have[a] for a in arrivals))

    block_output, input_grad = have["output"], have["input"]
    down_grad, up_grad, out_grad = have["down"], have["up"], have["out"]
    qkv_grad = jnp.transpose(have["qkv"], (1, 0, 2))
    vectors = jnp.sum(have["w"], axis=0)
    return (
        block_output,
        input_grad,
        qkv_grad,
        out_grad,
        up_grad,
        down_grad,
        vectors[0],
        vectors[1],
        vectors[2],
        vectors[3],
    )


def solution(mesh):
    return jax.shard_map(
        partial(local, mesh.shape["seq"], mesh.shape["head"]),
        mesh=mesh,
        in_specs=(
            P("seq", None),
            P(),
            P("seq"),
            P("seq"),
            P("seq", None),
            P(),
            P(None, None, "head"),
            P("head", None),
            P(None, "head"),
            P("head", None),
            P(),
            P(),
            P(),
            P(),
            P("seq", None),
        ),
        out_specs=(
            P("seq", None),
            P("seq", None),
            P("seq", None, "head"),
            P("head", "seq"),
            P("seq", "head"),
            P("head", "seq"),
            P("seq"),
            P("seq"),
            P("seq"),
            P("seq"),
        ),
        check_vma=False,
    )
```

```python
from functools import partial
import math

import jax
import jax.numpy as jnp
from jax import lax
from jax.experimental import pallas as pl
from jax.experimental.pallas import tpu as pltpu
from jax.sharding import PartitionSpec as P

HEAD_DIM = 128
F32 = jnp.float32
BF16 = jnp.bfloat16
MIB = 1 << 20
NN = ((1,), (0,))
NT = ((1,), (1,))
TN = ((0,), (0,))


def dot(a, b, contract=NN):
    return lax.dot_general(a, b, (contract, ((), ())), preferred_element_type=F32)


def call(body, grid, ins, outs, scratch=(), flops=0, special=0, after=(), prefetch=None):
    arrays = [array for array, _, _ in ins]
    specs = [pl.BlockSpec(block, index) for _, block, index in ins] + [pl.BlockSpec(memory_space=pl.ANY)] * len(after)
    shapes = [jax.ShapeDtypeStruct(shape, kind) for shape, kind, _, _ in outs]
    n_in, n_pre = len(ins), 0 if prefetch is None else 1

    def wrapped(*refs):
        body(*refs[: n_pre + n_in], *refs[n_pre + n_in + len(after) :])

    moved = sum(a.size * a.dtype.itemsize for a in arrays) + sum(s.size * s.dtype.itemsize for s in shapes)
    out_specs = [pl.BlockSpec(block, index) for _, _, block, index in outs]
    keys = dict(
        out_shape=shapes,
        compiler_params=pltpu.CompilerParams(vmem_limit_bytes=55 * MIB),
        cost_estimate=pl.CostEstimate(flops=0, bytes_accessed=0, transcendentals=0),
    )
    if prefetch is None:
        made = pl.pallas_call(
            wrapped, grid=grid, in_specs=specs, out_specs=out_specs, scratch_shapes=list(scratch), **keys
        )
        return made(*arrays, *after)
    spec = pltpu.PrefetchScalarGridSpec(
        num_scalar_prefetch=1, grid=grid, in_specs=specs, out_specs=out_specs, scratch_shapes=list(scratch)
    )
    return pl.pallas_call(wrapped, grid_spec=spec, **keys)(prefetch, *arrays, *after)


def gate(x, *after):
    def body(*refs):
        pass

    anywhere = pl.BlockSpec(memory_space=pl.ANY)
    return pl.pallas_call(
        body,
        in_specs=[anywhere] * (1 + len(after)),
        out_specs=anywhere,
        out_shape=jax.ShapeDtypeStruct(x.shape, x.dtype),
        input_output_aliases={0: 0},
        cost_estimate=pl.CostEstimate(flops=0, bytes_accessed=0, transcendentals=0),
    )(x, *after)


def block_matmul(picks, b, transposed=False, tile=512, received=None, after=()):
    rows, depth = picks[0][0].shape[0] // picks[0][2], picks[0][0].shape[1]
    width = b.shape[0] if transposed else b.shape[1]

    def body(x_ref, y_ref, b_ref, *rest):
        o_ref, p_ref, both = rest[-3:]

        @pl.when(pl.program_id(0) == 0)
        def _():
            both[:rows] = x_ref[...]
            both[rows:] = y_ref[...]

        result = dot(both[...], b_ref[...], NT if transposed else NN)
        o_ref[...] = result[:rows].astype(BF16)
        second = result[rows:]
        if received is not None:
            second += rest[0][...].astype(F32)
        p_ref[...] = second.astype(BF16)

    side = ((tile, depth), lambda j: (j, 0)) if transposed else ((depth, tile), lambda j: (0, j))
    more = [] if received is None else [(received, (rows, tile), lambda j: (0, j))]
    return call(
        body,
        (width // tile,),
        [(x, (rows, depth), lambda j, n=n: (n, 0)) for x, n, _ in picks] + [(b, *side)] + more,
        [((rows, width), BF16, (rows, tile), lambda j: (0, j))] * 2,
        [pltpu.VMEM((2 * rows, depth), BF16)],
        flops=4 * rows * width * depth,
        after=after,
    )


def project(pair, w3, after=()):
    rows, depth = pair[0].shape
    width = w3.shape[2]

    def body(x_ref, y_ref, w_ref, o_ref, both):
        @pl.when(pl.program_id(0) == 0)
        def _():
            both[:rows] = x_ref[...]
            both[rows:] = y_ref[...]

        o_ref[0] = dot(both[...], w_ref[0]).astype(BF16)

    return call(
        body,
        (3,),
        [(x, (rows, depth), lambda s: (0, 0)) for x in pair]
        + [(w3, (1, depth, width), lambda s: (s, 0, 0))],
        [((3, 2 * rows, width), BF16, (1, 2 * rows, width), lambda s: (s, 0, 0))],
        [pltpu.VMEM((2 * rows, depth), BF16)],
        flops=12 * rows * width * depth,
        after=after,
    )[0]


def project_back(g3, w3, picks, tile=512, received=None, after=()):
    width, depth, rows = g3.shape[2], w3.shape[1], g3.shape[1] // 4

    def body(x_ref, y_ref, w_ref, *rest):
        o_ref, p_ref, both = rest[-3:]

        @pl.when(pl.program_id(0) == 0)
        def _():
            both[:, :rows] = x_ref[...]
            both[:, rows:] = y_ref[...]

        total = dot(both[0], w_ref[0], NT)
        total += dot(both[1], w_ref[1], NT)
        total += dot(both[2], w_ref[2], NT)
        o_ref[...] = total[:rows].astype(BF16)
        second = total[rows:]
        if received is not None:
            second += rest[0][...].astype(F32)
        p_ref[...] = second.astype(BF16)

    more = [] if received is None else [(received, (rows, tile), lambda j: (0, j))]
    return call(
        body,
        (depth // tile,),
        [(g3, (3, rows, width), lambda j, n=n: (0, n, 0)) for n in picks]
        + [(w3, (3, tile, width), lambda j: (0, j, 0))]
        + more,
        [((rows, depth), BF16, (rows, tile), lambda j: (0, j))] * 2,
        [pltpu.VMEM((3, 2 * rows, width), BF16)],
        flops=12 * rows * width * depth,
        after=after,
    )


def mlp(normed, cot, w_up, w_down, tile=512, after=()):
    rows, depth = normed[0].shape
    width = w_up.shape[1]

    def body(n0, n1, c0, c1, u_ref, d_ref, act_ref, bar_ref, n_both, c_both):
        @pl.when(pl.program_id(0) == 0)
        def _():
            n_both[:rows] = n0[...]
            n_both[rows:] = n1[...]
            c_both[:rows] = c0[...]
            c_both[rows:] = c1[...]

        up = dot(n_both[...], u_ref[...])
        grad = dot(c_both[...], d_ref[...], NT)
        bell = jnp.exp(up * up * -0.5)
        t = 1.0 / (1.0 + (0.3275911 / math.sqrt(2.0)) * jnp.abs(up))
        poly = t * (
            0.127414796 + t * (-0.142248368 + t * (0.7107068705 + t * (-0.7265760135 + t * 0.5307027145)))
        )
        tail = poly * bell
        phi = jnp.where(up < 0.0, tail, 1.0 - tail)
        act_ref[...] = (up * phi).astype(BF16)
        slope = phi + up * bell * (1.0 / math.sqrt(2.0 * math.pi))
        bar_ref[...] = (slope * grad).astype(BF16)

    return call(
        body,
        (width // tile,),
        [(x, (rows, depth), lambda j: (0, 0)) for x in (*normed, *cot)]
        + [(w_up, (depth, tile), lambda j: (0, j)), (w_down, (tile, depth), lambda j: (j, 0))],
        [((2 * rows, width), BF16, (2 * rows, tile), lambda j: (0, j))] * 2,
        [pltpu.VMEM((2 * rows, depth), BF16)] * 2,
        flops=8 * rows * width * depth,
        special=4 * rows * width,
        after=after,
    )


def attend(picks, qkv, pos_col, start_col, pos_row, after=()):
    _, half, width = qkv[0].shape
    rows = half // 2
    heads = width // HEAD_DIM
    factor = 1.0 / math.sqrt(HEAD_DIM)

    def body(x_ref, y_ref, low_ref, high_ref, px_ref, py_ref, sx_ref, sy_ref, pr_ref, o_ref, kv):
        kv[:, :half] = low_ref[1:]
        kv[:, half:] = high_ref[1:]
        keys = pr_ref[...]
        at = jnp.concatenate([px_ref[...], py_ref[...]], axis=0)
        since = jnp.concatenate([sx_ref[...], sy_ref[...]], axis=0)
        bias = jnp.where((keys <= at) & (keys >= since), 0.0, -1e30)
        for head in range(heads):
            cols = slice(head * HEAD_DIM, (head + 1) * HEAD_DIM)
            q = jnp.concatenate([x_ref[0, :, cols], y_ref[0, :, cols]], axis=0)
            scores = dot(q, kv[0, :, cols], NT) * factor + bias
            peak = jnp.max(scores, axis=-1, keepdims=True)
            grown = jnp.exp(scores - peak)
            total = jnp.sum(grown, axis=-1, keepdims=True)
            o_ref[:, cols] = (dot(grown.astype(BF16), kv[1, :, cols]) * (1.0 / total)).astype(BF16)

    return call(
        body,
        (1,),
        [(qkv[n // 2], (1, rows, width), lambda i, n=n: (0, n % 2, 0)) for n in picks]
        + [
            (qkv[0], (3, half, width), lambda i: (0, 0, 0)),
            (qkv[1], (3, half, width), lambda i: (0, 0, 0)),
        ]
        + [(c, (rows, 1), lambda i, n=n: (n, 0)) for c in (pos_col, start_col) for n in picks]
        + [(pos_row, (1, 2 * half), lambda i: (0, 0))],
        [((half, width), BF16, (half, width), lambda i: (0, 0))],
        [pltpu.VMEM((2, 2 * half, width), BF16)],
        flops=8 * half * half * width,
        special=2 * heads * half * half,
        after=after,
    )[0]


def attend_back(qkv, bars, pos_col, pos_row, start_row, after=()):
    _, half, width = qkv[0].shape
    rows = 2 * half
    tile = rows // 2
    heads = width // HEAD_DIM
    factor = 1.0 / math.sqrt(HEAD_DIM)

    def body(low_ref, high_ref, g0, g1, g2, g3, pc_ref, pr_ref, sr_ref, o_ref, all_qkv, dk, dv, g_tile):
        step = pl.program_id(0)
        keys = pc_ref[...]
        seen = (keys <= pr_ref[...]) & (keys >= sr_ref[...])
        bias = jnp.where(seen, 0.0, -1e30)

        @pl.when(step == 0)
        def _():
            dk[...] = jnp.zeros_like(dk)
            dv[...] = jnp.zeros_like(dv)
            all_qkv[:, :half] = low_ref[...]
            all_qkv[:, half:] = high_ref[...]

        for number, (one, two) in enumerate(((g0, g1), (g2, g3))):

            @pl.when(step == number)
            def _():
                g_tile[: tile // 2] = one[...]
                g_tile[tile // 2 :] = two[...]

        here = pl.ds(pl.multiple_of(step * tile, tile), tile)
        for head in range(heads):
            cols = slice(head * HEAD_DIM, (head + 1) * HEAD_DIM)
            q, k, v, g = all_qkv[0, here, cols], all_qkv[1, :, cols], all_qkv[2, :, cols], g_tile[:, cols]
            scores = dot(k, q, NT) * factor + bias
            peak = jnp.max(scores, axis=0, keepdims=True)
            grown = jnp.exp(scores - peak)
            probs = grown * (1.0 / jnp.sum(grown, axis=0, keepdims=True))
            dv[:, cols] += dot(probs.astype(BF16), g)
            probs_bar = dot(v, g, NT)
            inner = jnp.sum(probs * probs_bar, axis=0, keepdims=True)
            scores_bar = (probs * (probs_bar - inner)).astype(BF16)
            dk[:, cols] += dot(scores_bar, q)
            dq = dot(scores_bar, k, TN) * factor
            o_ref[0, here, cols] = dq.astype(BF16)

        @pl.when(step == pl.num_programs(0) - 1)
        def _():
            o_ref[1] = (dk[...] * factor).astype(BF16)
            o_ref[2] = dv[...].astype(BF16)

    return call(
        body,
        (2,),
        [
            (qkv[0], (3, half, width), lambda i: (0, 0, 0)),
            (qkv[1], (3, half, width), lambda i: (0, 0, 0)),
            *[(bar, (tile // 2, width), lambda i: (0, 0)) for bar in bars],
            (pos_col, (rows, 1), lambda i: (0, 0)),
            (pos_row, (1, tile), lambda i: (0, i)),
            (start_row, (1, tile), lambda i: (0, i)),
        ],
        [((3, rows, width), BF16, (3, rows, width), lambda i: (0, 0, 0))],
        [
            pltpu.VMEM((3, rows, width), BF16),
            pltpu.VMEM((rows, width), F32),
            pltpu.VMEM((rows, width), F32),
            pltpu.VMEM((tile, width), BF16),
        ],
        flops=10 * rows * rows * width,
        special=heads * rows * rows,
        after=after,
    )[0]


def weight_grad(ids, lefts, rights, piece, block, received=None, after=()):
    count = ids.shape[0]
    rights = [r[None] if r.ndim == 2 else r for r in rights]
    part, column, pieces = piece
    width = rights[0].shape[2] // pieces
    halves = count // 2

    def body(ids_ref, *refs):
        left_refs, right_refs = refs[: len(lefts)], refs[len(lefts) : len(lefts) + len(rights)]
        rest = refs[len(lefts) + len(rights) :]
        left = jnp.concatenate([l[...] for l in left_refs], axis=0) if len(lefts) > 1 else left_refs[0][...]
        total, at = None, 0
        for r in right_refs:
            term = dot(left[at : at + r.shape[1]], r[0], TN)
            at += r.shape[1]
            total = term if total is None else total + term
        if received is None:
            rest[0][0] = total.astype(BF16)
            return
        total = (total + rest[0][0].astype(F32)).astype(BF16)
        i = pl.program_id(0)

        @pl.when(i < halves)
        def _():
            rest[1][0] = total

        @pl.when(i >= halves)
        def _():
            rest[2][0] = total

    ins = [(l, (l.shape[0], block), lambda i, ids: (0, ids[i])) for l in lefts]
    ins += [(r, (1, r.shape[1], width), lambda i, ids: (part, 0, column)) for r in rights]
    shape = (1, block, width)
    if received is None:
        outs = [((count, block, width), BF16, shape, lambda i, ids: (i, 0, 0))]
    else:
        ins.append((received, shape, lambda i, ids: (i, 0, 0)))
        outs = [
            ((halves, block, width), BF16, shape, lambda i, ids: (jnp.minimum(i, halves - 1), 0, 0)),
            ((halves, block, width), BF16, shape, lambda i, ids: (jnp.maximum(i - halves, 0), 0, 0)),
        ]
    rows = sum(l.shape[0] for l in lefts)
    result = call(body, (count,), ins, outs, flops=2 * rows * count * block * width, after=after, prefetch=ids)
    return result[0] if received is None else result


def add_halves(kept, received, after=()):
    count, block, width = kept.shape
    shape = (1, block, width)
    halves = count // 2

    def body(k_ref, r_ref, a_ref, b_ref):
        total = (k_ref[...].astype(F32) + r_ref[...].astype(F32)).astype(BF16)
        i = pl.program_id(0)

        @pl.when(i < halves)
        def _():
            a_ref[...] = total

        @pl.when(i >= halves)
        def _():
            b_ref[...] = total

    return call(
        body,
        (count,),
        [(x, shape, lambda i: (i, 0, 0)) for x in (kept, received)],
        [
            ((halves, block, width), BF16, shape, lambda i: (jnp.minimum(i, halves - 1), 0, 0)),
            ((halves, block, width), BF16, shape, lambda i: (jnp.maximum(i - halves, 0), 0, 0)),
        ],
        flops=kept.size,
        after=after,
    )


def add_last(terms, turn, parts=False, after=()):
    _, block, width = terms[0][0].shape
    count = len(terms)

    def body(*refs):
        for n in range(count):
            total = refs[2 * n][0].astype(F32) + refs[2 * n + 1][0].astype(F32)
            if parts:
                refs[-1][n] = total
            elif turn:
                refs[-1][n * width : (n + 1) * width] = total.T
            else:
                refs[-1][:, n * width : (n + 1) * width] = total

    shape = (count, block, width) if parts else (count * width, block) if turn else (block, count * width)
    return call(
        body,
        (1,),
        [(x, (1, block, width), lambda i: (0, 0, 0)) for pair in terms for x in pair],
        [(shape, F32, shape, lambda i: (0,) * len(shape))],
        flops=2 * block * width,
        after=after,
    )[0]


def unit_of(values):
    centre = values - jnp.mean(values, axis=-1, keepdims=True)
    scaling = lax.rsqrt(jnp.mean(centre * centre, axis=-1, keepdims=True) + 1e-05)
    return centre * scaling, scaling


def rowwise(body, rows_in, whole_in, outs, sums=0, tile=128, after=()):
    rows, depth = rows_in[0].shape
    return call(
        body,
        (rows // tile,),
        [(x, (tile, depth), lambda i: (i, 0)) for x in rows_in]
        + [(x, (1, depth), lambda i: (0, 0)) for x in whole_in],
        [((rows, depth), kind, (tile, depth), lambda i: (i, 0)) for kind in outs]
        + [((1, depth), F32, (1, depth), lambda i: (0, 0))] * sums,
        flops=20 * rows * depth,
        after=after,
    )


def norm_forward(values, gain, shift, after=()):
    def body(v_ref, g_ref, s_ref, o_ref):
        unit, _ = unit_of(v_ref[...].astype(F32))
        o_ref[...] = (unit * g_ref[...] + s_ref[...]).astype(BF16)

    return rowwise(body, [values], [gain, shift], [BF16], after=after)[0]


def sum_norm(base, terms, gain, shift, after=()):
    def body(b_ref, x_ref, y_ref, z_ref, g_ref, s_ref, h_ref, o_ref):
        total = x_ref[...].astype(F32) + y_ref[...].astype(F32) + z_ref[...].astype(F32)
        total = b_ref[...].astype(F32) + total
        h_ref[...] = total
        unit, _ = unit_of(total)
        o_ref[...] = (unit * g_ref[...] + s_ref[...]).astype(BF16)

    return rowwise(body, [base, *terms], [gain, shift], [F32, BF16], after=after)


def sum_low(base, terms, after=()):
    def body(b_ref, x_ref, y_ref, z_ref, o_ref):
        total = x_ref[...].astype(F32) + y_ref[...].astype(F32) + z_ref[...].astype(F32)
        o_ref[...] = (b_ref[...].astype(F32) + total).astype(BF16)

    return rowwise(body, [base, *terms], [], [BF16], after=after)[0]


def norm_back(base, values, terms, gain, keep, after=()):
    def body(b_ref, v_ref, x_ref, y_ref, z_ref, g_ref, o_ref, *rest):
        @pl.when(pl.program_id(0) == 0)
        def _():
            rest[-2][...] = jnp.zeros_like(rest[-2])
            rest[-1][...] = jnp.zeros_like(rest[-1])

        upstream = x_ref[...].astype(F32) + y_ref[...].astype(F32) + z_ref[...].astype(F32)
        unit, scaling = unit_of(v_ref[...].astype(F32))
        rest[-2][...] += jnp.sum(upstream * unit, axis=0, keepdims=True)
        rest[-1][...] += jnp.sum(upstream, axis=0, keepdims=True)
        scaled = upstream * g_ref[...]
        inner = (
            scaled
            - jnp.mean(scaled, axis=-1, keepdims=True)
            - unit * jnp.mean(scaled * unit, axis=-1, keepdims=True)
        )
        total = b_ref[...].astype(F32) + scaling * inner
        o_ref[...] = total.astype(BF16)
        if keep:
            rest[0][...] = total

    return rowwise(
        body, [base, values, *terms], [gain], [BF16, F32] if keep else [BF16], sums=2, after=after
    )


def place(index, pair, rows, so_far=None, after=()):
    block, depth = pair[0].shape
    tile = rows // 4

    def body(i_ref, x_ref, y_ref, *rest):
        where = lax.broadcasted_iota(jnp.int32, (tile, block), 0) + pl.program_id(0) * tile
        total = dot((where == i_ref[:, :block]).astype(BF16), x_ref[...])
        total += dot((where == i_ref[:, block:]).astype(BF16), y_ref[...])
        if so_far is not None:
            total += rest[0][...].astype(F32)
        rest[-1][...] = total.astype(BF16)

    more = [] if so_far is None else [(so_far, (tile, depth), lambda i: (i, 0))]
    return call(
        body,
        (rows // tile,),
        [
            (index, (1, 2 * block), lambda i: (0, 0)),
            (pair[0], (block, depth), lambda i: (0, 0)),
            (pair[1], (block, depth), lambda i: (0, 0)),
            *more,
        ],
        [((rows, depth), BF16, (tile, depth), lambda i: (i, 0))],
        flops=4 * rows * block * depth,
        after=after,
    )[0]


PLAN = (
    "fD",
    "fU",
    "KA",
    "KB",
    "BA",
    "NB",
    "GL",
    "BB",
    "GG",
    "sD",
    "GH",
    "fO",
    "sU",
    "OS",
    "AT",
    "aD",
    "KA1 O.y",
    "fQ",
    "KB1 x0",
    "fK U.z",
    "fV",
    "NB1 Q.y",
    "sO",
    "aU D.l",
    "sQ",
    "OL v",
    "aO",
    "sK",
    "aQ V.y",
    "sV",
    "aK",
    "GX U.l O.l V.z",
    "DE",
    "OH",
    "IL Q.l",
    "aV K.l",
    "GY w",
    "UE",
    "IH",
    "OE",
    "QE",
)


def local(
    n_seq,
    n_head,
    tokens,
    codebook,
    codes,
    modality,
    segments,
    sequence_source,
    w_qkv,
    w_out,
    w_up,
    w_down,
    norm1_gain,
    norm1_shift,
    norm2_gain,
    norm2_shift,
    cotangent,
):
    rows, depth = tokens.shape
    me, own = lax.axis_index("seq"), lax.axis_index("head")
    share = rows // n_seq // n_head
    quarter = rows // n_head
    w3 = jnp.transpose(w_qkv, (1, 0, 2))
    gain1, shift1, gain2, shift2 = [v[None] for v in (norm1_gain, norm1_shift, norm2_gain, norm2_shift)]

    def swap(x, flip, axis="head"):
        size = n_head if axis == "head" else n_seq
        return lax.ppermute(x, axis, [(i, i ^ flip) for i in range(size)])

    def exchange(x):
        return lax.all_to_all(x, "seq", split_axis=0, concat_axis=0, tiled=True)

    source = sequence_source.reshape(n_seq, rows)
    places = jnp.arange(rows, dtype=jnp.int32)
    groups = source // rows
    offsets = source % rows
    leaving = groups == me
    coming = lax.dynamic_index_in_dim(groups, me, 0) == jnp.arange(n_seq, dtype=jnp.int32)[:, None]
    upper = (places[:, None] <= places[None, :]).astype(BF16)
    counts = jnp.dot(
        jnp.concatenate([leaving, coming], axis=0).astype(BF16), upper, preferred_element_type=F32
    ).astype(jnp.int32)
    leaving_rank = jnp.where(leaving, counts[:n_seq] - 1, -1)
    coming_rank = jnp.where(coming, counts[n_seq:] - 1, -1)
    lanes = jnp.arange(share, dtype=jnp.int32)

    def listed(rank, value, blocks):
        wanted = (own ^ jnp.asarray(blocks, jnp.int32))[:, None] * share + lanes[None, :]
        hit = rank[None, :, None, :] == wanted[:, None, :, None]
        return jnp.sum(jnp.where(hit, value[None, :, None, :], 0), axis=-1).reshape(-1)

    sent = listed(leaving_rank, offsets, [0])
    pick = (sent[:, None] == places[None, :]).astype(BF16)
    code = jnp.where(modality == 1, codes, -1)
    sent_code = jnp.sum(jnp.where(sent[:, None] == places[None, :], code[None, :], 0), axis=-1)
    pick_code = (
        sent_code[:, None] == jnp.arange(codebook.shape[0], dtype=jnp.int32)[None, :]
    ).astype(BF16)
    leaving_embedded = (
        jnp.dot(pick, tokens, preferred_element_type=F32)
        + jnp.dot(pick_code, codebook, preferred_element_type=F32)
    ).astype(BF16)
    embedded = exchange(leaving_embedded)

    sent_across = listed(leaving_rank, offsets, [2])
    pick_across = (sent_across[:, None] == places[None, :]).astype(BF16)
    leaving_cot = jnp.concatenate(
        [
            jnp.dot(p, cotangent, preferred_element_type=F32).astype(BF16).reshape(n_seq, share, depth)
            for p in (pick, pick_across)
        ],
        axis=1,
    )
    came = exchange(leaving_cot)
    cot0, cot2 = [came[:, i * share : (i + 1) * share].reshape(quarter, depth) for i in range(2)]
    cot1, cot3 = swap(cot0, 1), swap(cot2, 1)

    sent_all = listed(leaving_rank, offsets, list(range(n_head)))
    segment_row = segments[0]
    begin = jnp.sum((segment_row[:, None] < segment_row[None, :]).astype(jnp.int32), axis=0)
    packed = listed(
        coming_rank, jnp.broadcast_to(begin * rows + places, (n_seq, rows)), list(range(n_head))
    )
    position, start = packed % rows, packed // rows
    pos_col, start_col, pos_row, start_row = position[:, None], start[:, None], position[None], start[None]

    n0 = norm_forward(embedded, gain1, shift1)
    n2 = swap(n0, 2)
    n1 = swap(n0, 1)
    qkv_low = project((n0, n1), w3)
    n2 = gate(n2, qkv_low)
    n3 = swap(n2, 1)
    qkv = (qkv_low, project((n2, n3), w3))
    mixed_out = attend((1, 3), qkv, pos_col, start_col, pos_row)
    a1, a3 = block_matmul(((mixed_out, 0, 2), (mixed_out, 1, 2)), w_out, tile=1024)
    mixed_in = attend((0, 2), qkv, pos_col, start_col, pos_row, after=(a1,))
    a0, passed = block_matmul(
        ((mixed_in, 0, 2), (mixed_in, 1, 2)), w_out, tile=1024, received=swap(a3, 1)
    )
    hidden_in, m0 = sum_norm(embedded, (a0, swap(a1, 1), swap(passed, 2)), gain2, shift2)

    m2 = swap(m0, 2)
    m1 = swap(m0, 1)
    act_low, bar_low = mlp((m0, m1), (cot0, cot1), w_up, w_down)
    m2 = gate(m2, act_low)
    m3 = swap(m2, 1)
    act_high, bar_high = mlp((m2, m3), (cot2, cot3), w_up, w_down)
    bars_out, bars_in = ((bar_low, 1, 2), (bar_high, 1, 2)), ((bar_low, 0, 2), (bar_high, 0, 2))
    acts_out, acts_in = ((act_low, 1, 2), (act_high, 1, 2)), ((act_low, 0, 2), (act_high, 0, 2))

    bits = n_seq.bit_length() - 1
    block = depth // n_seq

    def keep_order(order):
        kept = [0]
        for bit in reversed(order[1:]):
            kept = [k | 1 << bit for k in kept] + kept
        return jnp.asarray(kept, jnp.int32)

    def columns(blocks, ids):
        if block % 128 == 0:
            return blocks, ids, block
        picked = [jnp.take(b.reshape(-1, n_seq, block), ids, axis=1).reshape(b.shape[0], -1) for b in blocks]
        return picked, jnp.arange(n_seq // 2 * block // 128, dtype=jnp.int32), 128

    def first_term(grad, after=()):
        order, lefts, rights, piece = grad
        ids = me ^ (1 << order[0]) ^ keep_order(order)
        blocks, ids, size = columns(lefts, ids)
        made = weight_grad(ids, blocks, rights, piece, size, after=after)
        return swap(made, 1 << order[0], "seq"), made

    def second_term(grad, received, after=()):
        order, lefts, rights, piece = grad
        blocks, ids, size = columns(lefts, me ^ keep_order(order))
        send, keep = weight_grad(ids, blocks, rights, piece, size, received, after=after)
        send, keep = [x.reshape(n_seq // 4, block, x.shape[2]) for x in (send, keep)]
        return swap(send, 1 << order[1], "seq"), keep

    def next_terms(grad, received, keep, after=()):
        for bit in grad[0][2:]:
            send, keep = add_halves(keep, received, after=after)
            received = swap(send, 1 << bit, "seq")
        return received, keep

    straight = list(range(bits))
    turned = [1, 0] + straight[2:]
    cots = (cot0, cot1, cot2, cot3)
    normed_one, normed_two = (n0, n1, n2, n3), (m0, m1, m2, m3)

    acts, bars = (act_low, act_high), (bar_low, bar_high)
    have = {}
    grads = {
        "D": (straight, cots, acts, (0, 0, 1)),
        "U": (turned, normed_two, bars, (0, 0, 1)),
    }
    where = [sent_all[None, : 2 * quarter], sent_all[None, 2 * quarter :]]

    def first(name, after):
        have[name + ".y"], made = first_term(grads[name], after)
        return made

    def second(name, after):
        have[name + ".z"], have[name + ".k"] = second_term(grads[name], have[name + ".y"], after)
        return have[name + ".k"]

    def add(name, after):
        have[name + ".l"], have[name + ".m"] = next_terms(grads[name], have[name + ".z"], have[name + ".k"], after)
        return have[name + ".m"]

    def last(name):
        return have[name + ".l"], have[name + ".m"]

    def near_up(after):
        t1, t3 = block_matmul(bars_out, w_up, transposed=True, after=after)
        have["t1"], have["t3"] = swap(t1, 1), swap(t3, 1)
        return t1

    def near_branch(after):
        b1, b3 = block_matmul(acts_out, w_down, after=after)
        have["b1"], have["b3"] = swap(b1, 1), swap(b3, 1)
        return b1

    def far_up(after):
        have["t0"], passed = block_matmul(bars_in, w_up, transposed=True, received=have["t3"], after=after)
        have["t2"] = swap(passed, 2)
        return passed

    def far_branch(after):
        have["b0"], passed = block_matmul(acts_in, w_down, received=have["b3"], after=after)
        have["b2"] = swap(passed, 2)
        return passed

    def hidden(after):
        h0, have["hidden_bar"], have["gain_two"], have["shift_two"] = norm_back(
            cot0, hidden_in, (have["t0"], have["t1"], have["t2"]), gain2, True, after=after
        )
        have["h0"], have["h2"], have["h1"] = h0, swap(h0, 2), swap(h0, 1)
        return h0

    def context_low(after):
        have["g0"], have["g1"] = block_matmul(
            ((have["h0"], 0, 1), (have["h1"], 0, 1)), w_out, transposed=True, after=after
        )
        return have["g1"]

    def gate_hidden(after):
        have["h2"] = gate(have["h2"], *after)
        have["h3"] = swap(have["h2"], 1)
        grads["O"] = (
            straight,
            (have["h1"], have["h3"], have["h0"], have["h2"]),
            (mixed_out, mixed_in),
            (0, 0, 1),
        )
        return have["h2"]

    def context_high(after):
        have["g2"], have["g3"] = block_matmul(
            ((have["h2"], 0, 1), (have["h3"], 0, 1)), w_out, transposed=True, after=after
        )
        return have["g3"]

    def output(after):
        made = sum_low(hidden_in, (have["b0"], have["b1"], have["b2"]), after=after)
        home = exchange(made)
        have["x0"], have["x1"], have["x2"] = home, swap(home, 1), swap(home, 2)
        return made

    def attention(after):
        made = attend_back(
            qkv, [have[g] for g in ("g0", "g1", "g2", "g3")], pos_col, pos_row, start_row, after=after
        )
        for n, name in enumerate(("Q", "K", "V")):
            grads[name] = (straight, normed_one, (made,), (n, 0, 1))
        have["qkv_bar"] = made
        return made

    def near_input(after):
        u1, u3 = project_back(have["qkv_bar"], w3, (1, 3), after=after)
        have["u1"], have["u3"] = swap(u1, 1), swap(u3, 1)
        return u1

    def far_input(after):
        have["u0"], passed = project_back(have["qkv_bar"], w3, (0, 2), received=have["u3"], after=after)
        have["u2"] = swap(passed, 2)
        return passed

    def inputs(after):
        made, gain_one, shift_one = norm_back(
            have["hidden_bar"], embedded, (have["u0"], have["u1"], have["u2"]), gain1, False, after=after
        )
        home = exchange(made)
        have["y0"], have["y1"], have["y2"] = home, swap(home, 1), swap(home, 2)
        vectors = jnp.concatenate([gain_one, shift_one, have["gain_two"], have["shift_two"]], axis=0)
        vectors = vectors + swap(vectors, 1)
        have["v"] = vectors + swap(vectors, 2)
        have["w"] = exchange(jnp.transpose(have["v"].reshape(4, n_seq, block), (1, 0, 2)))
        return made

    def place_low(out, x, after):
        have[out] = place(where[0], (have[x + "0"], have[x + "1"]), rows, after=after)
        return have[out]

    def gate_across(x, after):
        have[x + "2"] = gate(have[x + "2"], *after)
        have[x + "3"] = swap(have[x + "2"], 1)
        return have[x + "2"]

    def place_high(out, x, after):
        have[out] = place(where[1], (have[x + "2"], have[x + "3"]), rows, have[out], after=after)
        return have[out]

    def down_end(after):
        have["down"] = add_last([last("D")], True, after=after)
        return have["down"]

    def up_end(after):
        have["up"] = add_last([last("U")], False, after=after)
        return have["up"]

    def out_end(after):
        have["out"] = add_last([last("O")], True, after=after)
        return have["out"]

    def qkv_end(after):
        have["qkv"] = add_last([last("Q"), last("K"), last("V")], False, True, after=after)
        return have["qkv"]

    steps = {
        "KA": near_up,
        "BA": near_branch,
        "KB": far_up,
        "NB": hidden,
        "GL": context_low,
        "BB": far_branch,
        "GG": gate_hidden,
        "GH": context_high,
        "OS": output,
        "AT": attention,
        "KA1": near_input,
        "KB1": far_input,
        "NB1": inputs,
        "OL": partial(place_low, "output", "x"),
        "GX": partial(gate_across, "x"),
        "OH": partial(place_high, "output", "x"),
        "IL": partial(place_low, "input", "y"),
        "GY": partial(gate_across, "y"),
        "IH": partial(place_high, "input", "y"),
        "DE": down_end,
        "UE": up_end,
        "OE": out_end,
        "QE": qkv_end,
    }
    for name in "DUOQKV":
        steps["f" + name] = partial(first, name)
        steps["s" + name] = partial(second, name)
        steps["a" + name] = partial(add, name)
    made = None
    for line in PLAN:
        step, *arrivals = line.split()
        after = () if made is None else (made,)
        made = steps[step](after + tuple(have[a] for a in arrivals))

    block_output, input_grad = have["output"], have["input"]
    down_grad, up_grad, out_grad = have["down"], have["up"], have["out"]
    qkv_grad = jnp.transpose(have["qkv"], (1, 0, 2))
    vectors = jnp.sum(have["w"], axis=0)
    return (
        block_output,
        input_grad,
        qkv_grad,
        out_grad,
        up_grad,
        down_grad,
        vectors[0],
        vectors[1],
        vectors[2],
        vectors[3],
    )


def solution(mesh):
    return jax.shard_map(
        partial(local, mesh.shape["seq"], mesh.shape["head"]),
        mesh=mesh,
        in_specs=(
            P("seq", None),
            P(),
            P("seq"),
            P("seq"),
            P("seq", None),
            P(),
            P(None, None, "head"),
            P("head", None),
            P(None, "head"),
            P("head", None),
            P(),
            P(),
            P(),
            P(),
            P("seq", None),
        ),
        out_specs=(
            P("seq", None),
            P("seq", None),
            P("seq", None, "head"),
            P("head", "seq"),
            P("seq", "head"),
            P("head", "seq"),
            P("seq"),
            P("seq"),
            P("seq"),
            P("seq"),
        ),
        check_vma=False,
    )
```

```python
from functools import partial
import math

import jax
import jax.numpy as jnp
from jax import lax
from jax.experimental import pallas as pl
from jax.experimental.pallas import tpu as pltpu
from jax.sharding import PartitionSpec as P

HEAD_DIM = 128
F32 = jnp.float32
BF16 = jnp.bfloat16
MIB = 1 << 20
NN = ((1,), (0,))
NT = ((1,), (1,))
TN = ((0,), (0,))


def dot(a, b, contract=NN):
    return lax.dot_general(a, b, (contract, ((), ())), preferred_element_type=F32)


def call(body, grid, ins, outs, scratch=(), flops=0, special=0, after=(), prefetch=None):
    arrays = [array for array, _, _ in ins]
    specs = [pl.BlockSpec(block, index) for _, block, index in ins] + [pl.BlockSpec(memory_space=pl.ANY)] * len(after)
    shapes = [jax.ShapeDtypeStruct(shape, kind) for shape, kind, _, _ in outs]
    n_in, n_pre = len(ins), 0 if prefetch is None else 1

    def wrapped(*refs):
        body(*refs[: n_pre + n_in], *refs[n_pre + n_in + len(after) :])

    moved = sum(a.size * a.dtype.itemsize for a in arrays) + sum(s.size * s.dtype.itemsize for s in shapes)
    out_specs = [pl.BlockSpec(block, index) for _, _, block, index in outs]
    keys = dict(
        out_shape=shapes,
        compiler_params=pltpu.CompilerParams(vmem_limit_bytes=55 * MIB),
        cost_estimate=pl.CostEstimate(flops=0, bytes_accessed=0, transcendentals=0),
    )
    if prefetch is None:
        made = pl.pallas_call(
            wrapped, grid=grid, in_specs=specs, out_specs=out_specs, scratch_shapes=list(scratch), **keys
        )
        return made(*arrays, *after)
    spec = pltpu.PrefetchScalarGridSpec(
        num_scalar_prefetch=1, grid=grid, in_specs=specs, out_specs=out_specs, scratch_shapes=list(scratch)
    )
    return pl.pallas_call(wrapped, grid_spec=spec, **keys)(prefetch, *arrays, *after)


def gate(x, *after):
    def body(*refs):
        pass

    anywhere = pl.BlockSpec(memory_space=pl.ANY)
    return pl.pallas_call(
        body,
        in_specs=[anywhere] * (1 + len(after)),
        out_specs=anywhere,
        out_shape=jax.ShapeDtypeStruct(x.shape, x.dtype),
        input_output_aliases={0: 0},
        cost_estimate=pl.CostEstimate(flops=0, bytes_accessed=0, transcendentals=0),
    )(x, *after)


def block_matmul(picks, b, transposed=False, tile=1024, received=None, after=()):
    rows, depth = picks[0][0].shape[0] // picks[0][2], picks[0][0].shape[1]
    width = b.shape[0] if transposed else b.shape[1]
    tile = min(tile, width)

    def body(x_ref, y_ref, b_ref, *rest):
        o_ref, p_ref, both = rest[-3:]

        @pl.when(pl.program_id(0) == 0)
        def _():
            both[:rows] = x_ref[...]
            both[rows:] = y_ref[...]

        result = dot(both[...], b_ref[...], NT if transposed else NN)
        o_ref[...] = result[:rows].astype(BF16)
        second = result[rows:]
        if received is not None:
            second += rest[0][...].astype(F32)
        p_ref[...] = second.astype(BF16)

    side = ((tile, depth), lambda j: (j, 0)) if transposed else ((depth, tile), lambda j: (0, j))
    more = [] if received is None else [(received, (rows, tile), lambda j: (0, j))]
    return call(
        body,
        (width // tile,),
        [(x, (rows, depth), lambda j, n=n: (n, 0)) for x, n, _ in picks] + [(b, *side)] + more,
        [((rows, width), BF16, (rows, tile), lambda j: (0, j))] * 2,
        [pltpu.VMEM((2 * rows, depth), BF16)],
        flops=4 * rows * width * depth,
        after=after,
    )


def project(pair, w3, after=()):
    rows, depth = pair[0].shape
    width = w3.shape[2]

    def body(x_ref, y_ref, w_ref, o_ref, both):
        @pl.when(pl.program_id(0) == 0)
        def _():
            both[:rows] = x_ref[...]
            both[rows:] = y_ref[...]

        o_ref[0] = dot(both[...], w_ref[0]).astype(BF16)

    return call(
        body,
        (3,),
        [(x, (rows, depth), lambda s: (0, 0)) for x in pair]
        + [(w3, (1, depth, width), lambda s: (s, 0, 0))],
        [((3, 2 * rows, width), BF16, (1, 2 * rows, width), lambda s: (s, 0, 0))],
        [pltpu.VMEM((2 * rows, depth), BF16)],
        flops=12 * rows * width * depth,
        after=after,
    )[0]


def project_back(g3, w3, picks, tile=512, received=None, after=()):
    width, depth, rows = g3.shape[2], w3.shape[1], g3.shape[1] // 4

    def body(x_ref, y_ref, w_ref, *rest):
        o_ref, p_ref, both = rest[-3:]

        @pl.when(pl.program_id(0) == 0)
        def _():
            both[:, :rows] = x_ref[...]
            both[:, rows:] = y_ref[...]

        total = dot(both[0], w_ref[0], NT)
        total += dot(both[1], w_ref[1], NT)
        total += dot(both[2], w_ref[2], NT)
        o_ref[...] = total[:rows].astype(BF16)
        second = total[rows:]
        if received is not None:
            second += rest[0][...].astype(F32)
        p_ref[...] = second.astype(BF16)

    more = [] if received is None else [(received, (rows, tile), lambda j: (0, j))]
    return call(
        body,
        (depth // tile,),
        [(g3, (3, rows, width), lambda j, n=n: (0, n, 0)) for n in picks]
        + [(w3, (3, tile, width), lambda j: (0, j, 0))]
        + more,
        [((rows, depth), BF16, (rows, tile), lambda j: (0, j))] * 2,
        [pltpu.VMEM((3, 2 * rows, width), BF16)],
        flops=12 * rows * width * depth,
        after=after,
    )


def mlp(normed, cot, w_up, w_down, tile=512, after=()):
    rows, depth = normed[0].shape
    width = w_up.shape[1]

    def body(n0, n1, c0, c1, u_ref, d_ref, act_ref, bar_ref, n_both, c_both):
        @pl.when(pl.program_id(0) == 0)
        def _():
            n_both[:rows] = n0[...]
            n_both[rows:] = n1[...]
            c_both[:rows] = c0[...]
            c_both[rows:] = c1[...]

        up = dot(n_both[...], u_ref[...])
        grad = dot(c_both[...], d_ref[...], NT)
        bell = jnp.exp(up * up * -0.5)
        t = 1.0 / (1.0 + (0.3275911 / math.sqrt(2.0)) * jnp.abs(up))
        poly = t * (
            0.127414796 + t * (-0.142248368 + t * (0.7107068705 + t * (-0.7265760135 + t * 0.5307027145)))
        )
        tail = poly * bell
        phi = jnp.where(up < 0.0, tail, 1.0 - tail)
        act_ref[...] = (up * phi).astype(BF16)
        slope = phi + up * bell * (1.0 / math.sqrt(2.0 * math.pi))
        bar_ref[...] = (slope * grad).astype(BF16)

    return call(
        body,
        (width // tile,),
        [(x, (rows, depth), lambda j: (0, 0)) for x in (*normed, *cot)]
        + [(w_up, (depth, tile), lambda j: (0, j)), (w_down, (tile, depth), lambda j: (j, 0))],
        [((2 * rows, width), BF16, (2 * rows, tile), lambda j: (0, j))] * 2,
        [pltpu.VMEM((2 * rows, depth), BF16)] * 2,
        flops=8 * rows * width * depth,
        special=4 * rows * width,
        after=after,
    )


def attend(picks, qkv, pos_col, start_col, pos_row, after=()):
    _, half, width = qkv[0].shape
    rows = half // 2
    heads = width // HEAD_DIM
    factor = 1.0 / math.sqrt(HEAD_DIM)

    def body(x_ref, y_ref, low_ref, high_ref, px_ref, py_ref, sx_ref, sy_ref, pr_ref, o_ref, kv):
        kv[:, :half] = low_ref[1:]
        kv[:, half:] = high_ref[1:]
        keys = pr_ref[...]
        at = jnp.concatenate([px_ref[...], py_ref[...]], axis=0)
        since = jnp.concatenate([sx_ref[...], sy_ref[...]], axis=0)
        bias = jnp.where((keys <= at) & (keys >= since), 0.0, -1e30)
        for head in range(heads):
            cols = slice(head * HEAD_DIM, (head + 1) * HEAD_DIM)
            q = jnp.concatenate([x_ref[0, :, cols], y_ref[0, :, cols]], axis=0)
            scores = dot(q, kv[0, :, cols], NT) * factor + bias
            peak = jnp.max(scores, axis=-1, keepdims=True)
            grown = jnp.exp(scores - peak)
            total = jnp.sum(grown, axis=-1, keepdims=True)
            o_ref[:, cols] = (dot(grown.astype(BF16), kv[1, :, cols]) * (1.0 / total)).astype(BF16)

    return call(
        body,
        (1,),
        [(qkv[n // 2], (1, rows, width), lambda i, n=n: (0, n % 2, 0)) for n in picks]
        + [
            (qkv[0], (3, half, width), lambda i: (0, 0, 0)),
            (qkv[1], (3, half, width), lambda i: (0, 0, 0)),
        ]
        + [(c, (rows, 1), lambda i, n=n: (n, 0)) for c in (pos_col, start_col) for n in picks]
        + [(pos_row, (1, 2 * half), lambda i: (0, 0))],
        [((half, width), BF16, (half, width), lambda i: (0, 0))],
        [pltpu.VMEM((2, 2 * half, width), BF16)],
        flops=8 * half * half * width,
        special=2 * heads * half * half,
        after=after,
    )[0]


def attend_back(qkv, bars, pos_col, pos_row, start_row, after=()):
    _, half, width = qkv[0].shape
    rows = 2 * half
    tile = rows // 2
    heads = width // HEAD_DIM
    factor = 1.0 / math.sqrt(HEAD_DIM)

    def body(low_ref, high_ref, g0, g1, g2, g3, pc_ref, pr_ref, sr_ref, o_ref, all_qkv, dk, dv, g_tile):
        step = pl.program_id(0)
        keys = pc_ref[...]
        seen = (keys <= pr_ref[...]) & (keys >= sr_ref[...])
        bias = jnp.where(seen, 0.0, -1e30)

        @pl.when(step == 0)
        def _():
            dk[...] = jnp.zeros_like(dk)
            dv[...] = jnp.zeros_like(dv)
            all_qkv[:, :half] = low_ref[...]
            all_qkv[:, half:] = high_ref[...]

        for number, (one, two) in enumerate(((g0, g1), (g2, g3))):

            @pl.when(step == number)
            def _():
                g_tile[: tile // 2] = one[...]
                g_tile[tile // 2 :] = two[...]

        here = pl.ds(pl.multiple_of(step * tile, tile), tile)
        for head in range(heads):
            cols = slice(head * HEAD_DIM, (head + 1) * HEAD_DIM)
            q, k, v, g = all_qkv[0, here, cols], all_qkv[1, :, cols], all_qkv[2, :, cols], g_tile[:, cols]
            scores = dot(k, q, NT) * factor + bias
            peak = jnp.max(scores, axis=0, keepdims=True)
            grown = jnp.exp(scores - peak)
            probs = grown * (1.0 / jnp.sum(grown, axis=0, keepdims=True))
            dv[:, cols] += dot(probs.astype(BF16), g)
            probs_bar = dot(v, g, NT)
            inner = jnp.sum(probs * probs_bar, axis=0, keepdims=True)
            scores_bar = (probs * (probs_bar - inner)).astype(BF16)
            dk[:, cols] += dot(scores_bar, q)
            dq = dot(scores_bar, k, TN) * factor
            o_ref[0, here, cols] = dq.astype(BF16)

        @pl.when(step == pl.num_programs(0) - 1)
        def _():
            o_ref[1] = (dk[...] * factor).astype(BF16)
            o_ref[2] = dv[...].astype(BF16)

    return call(
        body,
        (2,),
        [
            (qkv[0], (3, half, width), lambda i: (0, 0, 0)),
            (qkv[1], (3, half, width), lambda i: (0, 0, 0)),
            *[(bar, (tile // 2, width), lambda i: (0, 0)) for bar in bars],
            (pos_col, (rows, 1), lambda i: (0, 0)),
            (pos_row, (1, tile), lambda i: (0, i)),
            (start_row, (1, tile), lambda i: (0, i)),
        ],
        [((3, rows, width), BF16, (3, rows, width), lambda i: (0, 0, 0))],
        [
            pltpu.VMEM((3, rows, width), BF16),
            pltpu.VMEM((rows, width), F32),
            pltpu.VMEM((rows, width), F32),
            pltpu.VMEM((tile, width), BF16),
        ],
        flops=10 * rows * rows * width,
        special=heads * rows * rows,
        after=after,
    )[0]


def weight_grad(ids, lefts, rights, piece, block, received=None, after=()):
    count = ids.shape[0]
    rights = [r[None] if r.ndim == 2 else r for r in rights]
    part, column, pieces = piece
    width = rights[0].shape[2] // pieces
    halves = count // 2

    def body(ids_ref, *refs):
        left_refs, right_refs = refs[: len(lefts)], refs[len(lefts) : len(lefts) + len(rights)]
        rest = refs[len(lefts) + len(rights) :]
        left = jnp.concatenate([l[...] for l in left_refs], axis=0) if len(lefts) > 1 else left_refs[0][...]
        total, at = None, 0
        for r in right_refs:
            term = dot(left[at : at + r.shape[1]], r[0], TN)
            at += r.shape[1]
            total = term if total is None else total + term
        if received is None:
            rest[0][0] = total.astype(BF16)
            return
        total = (total + rest[0][0].astype(F32)).astype(BF16)
        i = pl.program_id(0)

        @pl.when(i < halves)
        def _():
            rest[1][0] = total

        @pl.when(i >= halves)
        def _():
            rest[2][0] = total

    ins = [(l, (l.shape[0], block), lambda i, ids: (0, ids[i])) for l in lefts]
    ins += [(r, (1, r.shape[1], width), lambda i, ids: (part, 0, column)) for r in rights]
    shape = (1, block, width)
    if received is None:
        outs = [((count, block, width), BF16, shape, lambda i, ids: (i, 0, 0))]
    else:
        ins.append((received, shape, lambda i, ids: (i, 0, 0)))
        outs = [
            ((halves, block, width), BF16, shape, lambda i, ids: (jnp.minimum(i, halves - 1), 0, 0)),
            ((halves, block, width), BF16, shape, lambda i, ids: (jnp.maximum(i - halves, 0), 0, 0)),
        ]
    rows = sum(l.shape[0] for l in lefts)
    result = call(body, (count,), ins, outs, flops=2 * rows * count * block * width, after=after, prefetch=ids)
    return result[0] if received is None else result


def add_halves(kept, received, after=()):
    count, block, width = kept.shape
    shape = (1, block, width)
    halves = count // 2

    def body(k_ref, r_ref, a_ref, b_ref):
        total = (k_ref[...].astype(F32) + r_ref[...].astype(F32)).astype(BF16)
        i = pl.program_id(0)

        @pl.when(i < halves)
        def _():
            a_ref[...] = total

        @pl.when(i >= halves)
        def _():
            b_ref[...] = total

    return call(
        body,
        (count,),
        [(x, shape, lambda i: (i, 0, 0)) for x in (kept, received)],
        [
            ((halves, block, width), BF16, shape, lambda i: (jnp.minimum(i, halves - 1), 0, 0)),
            ((halves, block, width), BF16, shape, lambda i: (jnp.maximum(i - halves, 0), 0, 0)),
        ],
        flops=kept.size,
        after=after,
    )


def add_last(terms, turn, parts=False, after=()):
    _, block, width = terms[0][0].shape
    count = len(terms)

    def body(*refs):
        for n in range(count):
            total = refs[2 * n][0].astype(F32) + refs[2 * n + 1][0].astype(F32)
            if parts:
                refs[-1][n] = total
            elif turn:
                refs[-1][n * width : (n + 1) * width] = total.T
            else:
                refs[-1][:, n * width : (n + 1) * width] = total

    shape = (count, block, width) if parts else (count * width, block) if turn else (block, count * width)
    return call(
        body,
        (1,),
        [(x, (1, block, width), lambda i: (0, 0, 0)) for pair in terms for x in pair],
        [(shape, F32, shape, lambda i: (0,) * len(shape))],
        flops=2 * block * width,
        after=after,
    )[0]


def unit_of(values):
    centre = values - jnp.mean(values, axis=-1, keepdims=True)
    scaling = lax.rsqrt(jnp.mean(centre * centre, axis=-1, keepdims=True) + 1e-05)
    return centre * scaling, scaling


def rowwise(body, rows_in, whole_in, outs, sums=0, tile=128, after=()):
    rows, depth = rows_in[0].shape
    return call(
        body,
        (rows // tile,),
        [(x, (tile, depth), lambda i: (i, 0)) for x in rows_in]
        + [(x, (1, depth), lambda i: (0, 0)) for x in whole_in],
        [((rows, depth), kind, (tile, depth), lambda i: (i, 0)) for kind in outs]
        + [((1, depth), F32, (1, depth), lambda i: (0, 0))] * sums,
        flops=20 * rows * depth,
        after=after,
    )


def norm_forward(values, gain, shift, after=()):
    def body(v_ref, g_ref, s_ref, o_ref):
        unit, _ = unit_of(v_ref[...].astype(F32))
        o_ref[...] = (unit * g_ref[...] + s_ref[...]).astype(BF16)

    return rowwise(body, [values], [gain, shift], [BF16], after=after)[0]


def sum_norm(base, terms, gain, shift, after=()):
    def body(b_ref, x_ref, y_ref, z_ref, g_ref, s_ref, h_ref, o_ref):
        total = x_ref[...].astype(F32) + y_ref[...].astype(F32) + z_ref[...].astype(F32)
        total = b_ref[...].astype(F32) + total
        h_ref[...] = total
        unit, _ = unit_of(total)
        o_ref[...] = (unit * g_ref[...] + s_ref[...]).astype(BF16)

    return rowwise(body, [base, *terms], [gain, shift], [F32, BF16], after=after)


def sum_low(base, terms, after=()):
    def body(b_ref, x_ref, y_ref, z_ref, o_ref):
        total = x_ref[...].astype(F32) + y_ref[...].astype(F32) + z_ref[...].astype(F32)
        o_ref[...] = (b_ref[...].astype(F32) + total).astype(BF16)

    return rowwise(body, [base, *terms], [], [BF16], after=after)[0]


def norm_back(base, values, terms, gain, keep, after=()):
    def body(b_ref, v_ref, x_ref, y_ref, z_ref, g_ref, o_ref, *rest):
        @pl.when(pl.program_id(0) == 0)
        def _():
            rest[-2][...] = jnp.zeros_like(rest[-2])
            rest[-1][...] = jnp.zeros_like(rest[-1])

        upstream = x_ref[...].astype(F32) + y_ref[...].astype(F32) + z_ref[...].astype(F32)
        unit, scaling = unit_of(v_ref[...].astype(F32))
        rest[-2][...] += jnp.sum(upstream * unit, axis=0, keepdims=True)
        rest[-1][...] += jnp.sum(upstream, axis=0, keepdims=True)
        scaled = upstream * g_ref[...]
        inner = (
            scaled
            - jnp.mean(scaled, axis=-1, keepdims=True)
            - unit * jnp.mean(scaled * unit, axis=-1, keepdims=True)
        )
        total = b_ref[...].astype(F32) + scaling * inner
        o_ref[...] = total.astype(BF16)
        if keep:
            rest[0][...] = total

    return rowwise(
        body, [base, values, *terms], [gain], [BF16, F32] if keep else [BF16], sums=2, after=after
    )


def place(index, pair, rows, so_far=None, after=()):
    block, depth = pair[0].shape
    tile = rows // 4

    def body(i_ref, x_ref, y_ref, *rest):
        where = lax.broadcasted_iota(jnp.int32, (tile, block), 0) + pl.program_id(0) * tile
        total = dot((where == i_ref[:, :block]).astype(BF16), x_ref[...])
        total += dot((where == i_ref[:, block:]).astype(BF16), y_ref[...])
        if so_far is not None:
            total += rest[0][...].astype(F32)
        rest[-1][...] = total.astype(BF16)

    more = [] if so_far is None else [(so_far, (tile, depth), lambda i: (i, 0))]
    return call(
        body,
        (rows // tile,),
        [
            (index, (1, 2 * block), lambda i: (0, 0)),
            (pair[0], (block, depth), lambda i: (0, 0)),
            (pair[1], (block, depth), lambda i: (0, 0)),
            *more,
        ],
        [((rows, depth), BF16, (tile, depth), lambda i: (i, 0))],
        flops=4 * rows * block * depth,
        after=after,
    )[0]


PLAN = (
    "fD",
    "fU",
    "KA",
    "KB",
    "BA",
    "NB",
    "GL",
    "BB",
    "GG",
    "sD",
    "GH",
    "fO",
    "sU",
    "OS",
    "AT",
    "aD",
    "KA1 O.y",
    "fQ",
    "KB1 x0",
    "fK U.z",
    "fV",
    "NB1 Q.y",
    "sO",
    "aU D.l",
    "sQ",
    "OL v",
    "aO",
    "sK",
    "aQ V.y",
    "sV",
    "aK",
    "GX U.l O.l V.z",
    "DE",
    "OH",
    "IL Q.l",
    "aV K.l",
    "GY w",
    "UE",
    "IH",
    "OE",
    "QE",
)


def local(
    n_seq,
    n_head,
    tokens,
    codebook,
    codes,
    modality,
    segments,
    sequence_source,
    w_qkv,
    w_out,
    w_up,
    w_down,
    norm1_gain,
    norm1_shift,
    norm2_gain,
    norm2_shift,
    cotangent,
):
    rows, depth = tokens.shape
    me, own = lax.axis_index("seq"), lax.axis_index("head")
    share = rows // n_seq // n_head
    quarter = rows // n_head
    w3 = jnp.transpose(w_qkv, (1, 0, 2))
    gain1, shift1, gain2, shift2 = [v[None] for v in (norm1_gain, norm1_shift, norm2_gain, norm2_shift)]

    def swap(x, flip, axis="head"):
        size = n_head if axis == "head" else n_seq
        return lax.ppermute(x, axis, [(i, i ^ flip) for i in range(size)])

    def exchange(x):
        return lax.all_to_all(x, "seq", split_axis=0, concat_axis=0, tiled=True)

    source = sequence_source.reshape(n_seq, rows)
    places = jnp.arange(rows, dtype=jnp.int32)
    groups = source // rows
    offsets = source % rows
    leaving = groups == me
    coming = lax.dynamic_index_in_dim(groups, me, 0) == jnp.arange(n_seq, dtype=jnp.int32)[:, None]
    upper = (places[:, None] <= places[None, :]).astype(BF16)
    counts = jnp.dot(
        jnp.concatenate([leaving, coming], axis=0).astype(BF16), upper, preferred_element_type=F32
    ).astype(jnp.int32)
    leaving_rank = jnp.where(leaving, counts[:n_seq] - 1, -1)
    coming_rank = jnp.where(coming, counts[n_seq:] - 1, -1)
    lanes = jnp.arange(share, dtype=jnp.int32)

    def listed(rank, value, blocks):
        wanted = (own ^ jnp.asarray(blocks, jnp.int32))[:, None] * share + lanes[None, :]
        hit = rank[None, :, None, :] == wanted[:, None, :, None]
        return jnp.sum(jnp.where(hit, value[None, :, None, :], 0), axis=-1).reshape(-1)

    sent = listed(leaving_rank, offsets, [0])
    pick = (sent[:, None] == places[None, :]).astype(BF16)
    code = jnp.where(modality == 1, codes, -1)
    sent_code = jnp.sum(jnp.where(sent[:, None] == places[None, :], code[None, :], 0), axis=-1)
    pick_code = (
        sent_code[:, None] == jnp.arange(codebook.shape[0], dtype=jnp.int32)[None, :]
    ).astype(BF16)
    leaving_embedded = (
        jnp.dot(pick, tokens, preferred_element_type=F32)
        + jnp.dot(pick_code, codebook, preferred_element_type=F32)
    ).astype(BF16)
    embedded = exchange(leaving_embedded)

    sent_across = listed(leaving_rank, offsets, [2])
    pick_across = (sent_across[:, None] == places[None, :]).astype(BF16)
    leaving_cot = jnp.concatenate(
        [
            jnp.dot(p, cotangent, preferred_element_type=F32).astype(BF16).reshape(n_seq, share, depth)
            for p in (pick, pick_across)
        ],
        axis=1,
    )
    came = exchange(leaving_cot)
    cot0, cot2 = [came[:, i * share : (i + 1) * share].reshape(quarter, depth) for i in range(2)]
    cot1, cot3 = swap(cot0, 1), swap(cot2, 1)

    sent_all = listed(leaving_rank, offsets, list(range(n_head)))
    segment_row = segments[0]
    begin = jnp.sum((segment_row[:, None] < segment_row[None, :]).astype(jnp.int32), axis=0)
    packed = listed(
        coming_rank, jnp.broadcast_to(begin * rows + places, (n_seq, rows)), list(range(n_head))
    )
    position, start = packed % rows, packed // rows
    pos_col, start_col, pos_row, start_row = position[:, None], start[:, None], position[None], start[None]

    n0 = norm_forward(embedded, gain1, shift1)
    n2 = swap(n0, 2)
    n1 = swap(n0, 1)
    qkv_low = project((n0, n1), w3)
    n2 = gate(n2, qkv_low)
    n3 = swap(n2, 1)
    qkv = (qkv_low, project((n2, n3), w3))
    mixed_out = attend((1, 3), qkv, pos_col, start_col, pos_row)
    a1, a3 = block_matmul(((mixed_out, 0, 2), (mixed_out, 1, 2)), w_out)
    mixed_in = attend((0, 2), qkv, pos_col, start_col, pos_row, after=(a1,))
    a0, passed = block_matmul(
        ((mixed_in, 0, 2), (mixed_in, 1, 2)), w_out, received=swap(a3, 1)
    )
    hidden_in, m0 = sum_norm(embedded, (a0, swap(a1, 1), swap(passed, 2)), gain2, shift2)

    m2 = swap(m0, 2)
    m1 = swap(m0, 1)
    act_low, bar_low = mlp((m0, m1), (cot0, cot1), w_up, w_down)
    m2 = gate(m2, act_low)
    m3 = swap(m2, 1)
    act_high, bar_high = mlp((m2, m3), (cot2, cot3), w_up, w_down)
    bars_out, bars_in = ((bar_low, 1, 2), (bar_high, 1, 2)), ((bar_low, 0, 2), (bar_high, 0, 2))
    acts_out, acts_in = ((act_low, 1, 2), (act_high, 1, 2)), ((act_low, 0, 2), (act_high, 0, 2))

    bits = n_seq.bit_length() - 1
    block = depth // n_seq

    def keep_order(order):
        kept = [0]
        for bit in reversed(order[1:]):
            kept = [k | 1 << bit for k in kept] + kept
        return jnp.asarray(kept, jnp.int32)

    def columns(blocks, ids):
        if block % 128 == 0:
            return blocks, ids, block
        picked = [jnp.take(b.reshape(-1, n_seq, block), ids, axis=1).reshape(b.shape[0], -1) for b in blocks]
        return picked, jnp.arange(n_seq // 2 * block // 128, dtype=jnp.int32), 128

    def first_term(grad, after=()):
        order, lefts, rights, piece = grad
        ids = me ^ (1 << order[0]) ^ keep_order(order)
        blocks, ids, size = columns(lefts, ids)
        made = weight_grad(ids, blocks, rights, piece, size, after=after)
        return swap(made, 1 << order[0], "seq"), made

    def second_term(grad, received, after=()):
        order, lefts, rights, piece = grad
        blocks, ids, size = columns(lefts, me ^ keep_order(order))
        send, keep = weight_grad(ids, blocks, rights, piece, size, received, after=after)
        send, keep = [x.reshape(n_seq // 4, block, x.shape[2]) for x in (send, keep)]
        return swap(send, 1 << order[1], "seq"), keep

    def next_terms(grad, received, keep, after=()):
        for bit in grad[0][2:]:
            send, keep = add_halves(keep, received, after=after)
            received = swap(send, 1 << bit, "seq")
        return received, keep

    straight = list(range(bits))
    turned = [1, 0] + straight[2:]
    cots = (cot0, cot1, cot2, cot3)
    normed_one, normed_two = (n0, n1, n2, n3), (m0, m1, m2, m3)

    acts, bars = (act_low, act_high), (bar_low, bar_high)
    have = {}
    grads = {
        "D": (straight, cots, acts, (0, 0, 1)),
        "U": (turned, normed_two, bars, (0, 0, 1)),
    }
    where = [sent_all[None, : 2 * quarter], sent_all[None, 2 * quarter :]]

    def first(name, after):
        have[name + ".y"], made = first_term(grads[name], after)
        return made

    def second(name, after):
        have[name + ".z"], have[name + ".k"] = second_term(grads[name], have[name + ".y"], after)
        return have[name + ".k"]

    def add(name, after):
        have[name + ".l"], have[name + ".m"] = next_terms(grads[name], have[name + ".z"], have[name + ".k"], after)
        return have[name + ".m"]

    def last(name):
        return have[name + ".l"], have[name + ".m"]

    def near_up(after):
        t1, t3 = block_matmul(bars_out, w_up, transposed=True, after=after)
        have["t1"], have["t3"] = swap(t1, 1), swap(t3, 1)
        return t1

    def near_branch(after):
        b1, b3 = block_matmul(acts_out, w_down, after=after)
        have["b1"], have["b3"] = swap(b1, 1), swap(b3, 1)
        return b1

    def far_up(after):
        have["t0"], passed = block_matmul(bars_in, w_up, transposed=True, received=have["t3"], after=after)
        have["t2"] = swap(passed, 2)
        return passed

    def far_branch(after):
        have["b0"], passed = block_matmul(acts_in, w_down, received=have["b3"], after=after)
        have["b2"] = swap(passed, 2)
        return passed

    def hidden(after):
        h0, have["hidden_bar"], have["gain_two"], have["shift_two"] = norm_back(
            cot0, hidden_in, (have["t0"], have["t1"], have["t2"]), gain2, True, after=after
        )
        have["h0"], have["h2"], have["h1"] = h0, swap(h0, 2), swap(h0, 1)
        return h0

    def context_low(after):
        have["g0"], have["g1"] = block_matmul(
            ((have["h0"], 0, 1), (have["h1"], 0, 1)), w_out, transposed=True, after=after
        )
        return have["g1"]

    def gate_hidden(after):
        have["h2"] = gate(have["h2"], *after)
        have["h3"] = swap(have["h2"], 1)
        grads["O"] = (
            straight,
            (have["h1"], have["h3"], have["h0"], have["h2"]),
            (mixed_out, mixed_in),
            (0, 0, 1),
        )
        return have["h2"]

    def context_high(after):
        have["g2"], have["g3"] = block_matmul(
            ((have["h2"], 0, 1), (have["h3"], 0, 1)), w_out, transposed=True, after=after
        )
        return have["g3"]

    def output(after):
        made = sum_low(hidden_in, (have["b0"], have["b1"], have["b2"]), after=after)
        home = exchange(made)
        have["x0"], have["x1"], have["x2"] = home, swap(home, 1), swap(home, 2)
        return made

    def attention(after):
        made = attend_back(
            qkv, [have[g] for g in ("g0", "g1", "g2", "g3")], pos_col, pos_row, start_row, after=after
        )
        for n, name in enumerate(("Q", "K", "V")):
            grads[name] = (straight, normed_one, (made,), (n, 0, 1))
        have["qkv_bar"] = made
        return made

    def near_input(after):
        u1, u3 = project_back(have["qkv_bar"], w3, (1, 3), after=after)
        have["u1"], have["u3"] = swap(u1, 1), swap(u3, 1)
        return u1

    def far_input(after):
        have["u0"], passed = project_back(have["qkv_bar"], w3, (0, 2), received=have["u3"], after=after)
        have["u2"] = swap(passed, 2)
        return passed

    def inputs(after):
        made, gain_one, shift_one = norm_back(
            have["hidden_bar"], embedded, (have["u0"], have["u1"], have["u2"]), gain1, False, after=after
        )
        home = exchange(made)
        have["y0"], have["y1"], have["y2"] = home, swap(home, 1), swap(home, 2)
        vectors = jnp.concatenate([gain_one, shift_one, have["gain_two"], have["shift_two"]], axis=0)
        vectors = vectors + swap(vectors, 1)
        have["v"] = vectors + swap(vectors, 2)
        have["w"] = exchange(jnp.transpose(have["v"].reshape(4, n_seq, block), (1, 0, 2)))
        return made

    def place_low(out, x, after):
        have[out] = place(where[0], (have[x + "0"], have[x + "1"]), rows, after=after)
        return have[out]

    def gate_across(x, after):
        have[x + "2"] = gate(have[x + "2"], *after)
        have[x + "3"] = swap(have[x + "2"], 1)
        return have[x + "2"]

    def place_high(out, x, after):
        have[out] = place(where[1], (have[x + "2"], have[x + "3"]), rows, have[out], after=after)
        return have[out]

    def down_end(after):
        have["down"] = add_last([last("D")], True, after=after)
        return have["down"]

    def up_end(after):
        have["up"] = add_last([last("U")], False, after=after)
        return have["up"]

    def out_end(after):
        have["out"] = add_last([last("O")], True, after=after)
        return have["out"]

    def qkv_end(after):
        have["qkv"] = add_last([last("Q"), last("K"), last("V")], False, True, after=after)
        return have["qkv"]

    steps = {
        "KA": near_up,
        "BA": near_branch,
        "KB": far_up,
        "NB": hidden,
        "GL": context_low,
        "BB": far_branch,
        "GG": gate_hidden,
        "GH": context_high,
        "OS": output,
        "AT": attention,
        "KA1": near_input,
        "KB1": far_input,
        "NB1": inputs,
        "OL": partial(place_low, "output", "x"),
        "GX": partial(gate_across, "x"),
        "OH": partial(place_high, "output", "x"),
        "IL": partial(place_low, "input", "y"),
        "GY": partial(gate_across, "y"),
        "IH": partial(place_high, "input", "y"),
        "DE": down_end,
        "UE": up_end,
        "OE": out_end,
        "QE": qkv_end,
    }
    for name in "DUOQKV":
        steps["f" + name] = partial(first, name)
        steps["s" + name] = partial(second, name)
        steps["a" + name] = partial(add, name)
    made = None
    for line in PLAN:
        step, *arrivals = line.split()
        after = () if made is None else (made,)
        made = steps[step](after + tuple(have[a] for a in arrivals))

    block_output, input_grad = have["output"], have["input"]
    down_grad, up_grad, out_grad = have["down"], have["up"], have["out"]
    qkv_grad = jnp.transpose(have["qkv"], (1, 0, 2))
    vectors = jnp.sum(have["w"], axis=0)
    return (
        block_output,
        input_grad,
        qkv_grad,
        out_grad,
        up_grad,
        down_grad,
        vectors[0],
        vectors[1],
        vectors[2],
        vectors[3],
    )


def solution(mesh):
    return jax.shard_map(
        partial(local, mesh.shape["seq"], mesh.shape["head"]),
        mesh=mesh,
        in_specs=(
            P("seq", None),
            P(),
            P("seq"),
            P("seq"),
            P("seq", None),
            P(),
            P(None, None, "head"),
            P("head", None),
            P(None, "head"),
            P("head", None),
            P(),
            P(),
            P(),
            P(),
            P("seq", None),
        ),
        out_specs=(
            P("seq", None),
            P("seq", None),
            P("seq", None, "head"),
            P("head", "seq"),
            P("seq", "head"),
            P("head", "seq"),
            P("seq"),
            P("seq"),
            P("seq"),
            P("seq"),
        ),
        check_vma=False,
    )
```
